32 devices in a mesh: grp: 2 (over x), ep: 16 (over z, y, core).
Axes of the slice: x: 2, y: 2, z: 4, core: 2. Of those that a mesh axis runs over, the one named last changes fastest.
Arguments:
- tokens: bfloat16 [4096, 2048], P(('grp', 'ep')), parts along dimension 0, may hold values from -6 to 6
- cotangent: bfloat16 [4096, 2048], P(('grp', 'ep')), parts along dimension 0, may hold values from -6 to 6
- route_ids: int32 [4096, 8], P(('grp', 'ep')), parts along dimension 0, may hold values from 0 to 15, all different within a row; in each aligned block of 128 rows (0 to 127, 128 to 255, ...) at most 96 rows name the same one
- route_weights: float32 [4096, 8], P(('grp', 'ep')), parts along dimension 0, may hold values from 0.05 to 1
- owner: int32 [32], P('grp'), parts along dimension 0, may hold values from 0 to 15, each once
- base_joined: bfloat16 [16, 2048, 768], P('ep'), may hold values from -0.125 to 0.125
- base_down: bfloat16 [16, 384, 2048], P('ep'), may hold values from -0.3125 to 0.3125
- master: float32 [32, 167936], P('grp', 'ep'), parts along dimension 0, may hold values from -0.3 to 0.3
- moment: float32 [32, 167936], P('grp', 'ep'), parts along dimension 0, may hold values from -0.6 to 0.6
- second: float32 [32, 167936], P('grp', 'ep'), parts along dimension 0, may hold values from 0.003 to 0.3
- step_rows: bfloat16 [4, 256, 2048], P(None, ('grp', 'ep')), parts along dimension 1, may hold values from -6 to 6
- step_ids: int32 [4, 256, 8], P(None, ('grp', 'ep')), parts along dimension 1, may hold values from 0 to 15, all different within a row; in each aligned block of 8 rows (0 to 7, 8 to 15, ..., all dimensions but the last counted through in order) at most 6 rows name the same one
- step_weights: float32 [4, 256, 8], P(None, ('grp', 'ep')), parts along dimension 1, may hold values from 0.05 to 1
Outputs:
- updated: float32 [32, 167936], P('grp', 'ep'), parts along dimension 0
- decoded: bfloat16 [4, 256, 2048], P(None, ('grp', 'ep')), parts along dimension 1
The draws below stay inside these ranges and needn't reach their ends.
There are 2 independent parts, one for each index of `grp`. The reference program is written for one: setup_inputs(seed, part) draws one part's arguments, and reference() takes and returns one part's arrays. A program takes and returns all parts, laid end to end along the dimension named above; an argument that names none is the same for every part. Nothing has to cross between parts.
Inputs may be any that keep to these rules, and one draw needn't show every extreme that they name: `route_ids`: each row names 8 different experts; in the rows of one device no expert is named more than 96 times, a bound that some block reaches. `step_ids`: each row names 8 different experts; in the rows of one device in one step no expert is named more than 6 times, a bound that some block reaches. `owner`: A permutation of the devices.
All inputs are finite; a program needn't handle non-finite values.
Results may differ from the reference program's by a relative error of at most 0.012.
The reference program's roundings to bfloat16 on the way count: a program that leaves them out, or rounds other values in their place, can miss the bound.
Values may be sent and summed in bfloat16 or wider, within the bound.
A program may use at most 128 MiB of HBM per device.

```python
import math
import jax
import jax.numpy as jnp
import numpy as np
from jax import lax

D = 2048
FF = 384
RANK = 32
TOPK = 8
STEPS = 4
TOK_DEV = 128
DEC_DEV = 8
EXPERTS = 16
CAP = 96
DCAP = 6
PFLAT = 167936
TOKENS = 2048
DTOK = 128
N_EP = 16


def strengthened(entries, rng, source, target, blocks, factor):
    def block_of(position):
        return (jnp.arange(entries.shape[position]) // (entries.shape[position] // blocks)).reshape((-1,) + (1,) * (entries.ndim - 1 - position))

    first = jax.random.permutation(rng, blocks)[block_of(target)]
    other_side = (block_of(target) + blocks // 2) % blocks
    return jnp.where((block_of(source) == first) | (block_of(source) == other_side), factor * entries, entries)


def block_scale(own_key, shape, pieces, least, top_value):
    def one(axis_at, shards_of):
        heights = jax.random.uniform(jax.random.fold_in(jax.random.fold_in(own_key, 6), axis_at), (shards_of,), jnp.float32, least / len(pieces), top_value / len(pieces))
        return jnp.repeat(jnp.exp(heights), shape[axis_at] // shards_of).reshape((-1,) + (1,) * (len(shape) - axis_at - 1))

    level = one(*pieces[0])
    for cut in pieces[1:]:
        level = level * one(*cut)
    return level


def routed_block(rng, own, number, rows, amount, top, reach, slope):
    ranking = jax.random.permutation(rng, amount)
    heavy_load, usual = load_shares(amount, rows * top, reach, slope, True), load_shares(amount, rows * top, reach, slope, False)
    places = jnp.arange(amount)

    def named(tallies, rotation):
        used = int((tallies > 0).sum())
        fixed = max(1, used // 4)
        moved = fixed + (places - fixed + rotation * (used - fixed)) % max(1, amount - fixed)
        return jnp.zeros((amount,), jnp.int32).at[ranking[jnp.where(places < fixed, places, moved)]].set(jnp.asarray(tallies, jnp.int32))

    tallies = jnp.where(number % 4 == 0, named(heavy_load, number // 4), named(usual, number - number // 4 - 1))
    mixed = jax.random.permutation(jax.random.fold_in(own, 3), amount)
    giver, sink = mixed[0:amount // 2 * 2:2], mixed[1:amount // 2 * 2:2]
    slack = jnp.minimum(tallies[giver] - 1, reach - tallies[sink]) // 2
    slack = jnp.where((giver == ranking[0]) | (sink == ranking[0]) | (tallies[sink] == 0), 0, jnp.maximum(slack, 0))
    moved = jax.random.randint(jax.random.fold_in(own, 4), (amount // 2,), 0, 1 << 20) % (slack + 1)
    tallies = tallies.at[giver].add(-moved).at[sink].add(moved)
    items = jnp.searchsorted(jnp.cumsum(tallies), jnp.arange(rows * top), side="right").astype(jnp.int32)
    grid = items.reshape(top, rows).T
    grid = grid[jax.random.permutation(jax.random.fold_in(own, 1), rows)]
    rotation = jax.random.randint(jax.random.fold_in(own, 2), (rows, 1), 0, top)
    return jnp.take_along_axis(grid, (jnp.arange(top)[None, :] + rotation) % top, axis=1)


def load_shares(count, total, bound, skew, full):
    portions = [(1 << 20) // math.isqrt(standing ** skew) + 1 for standing in range(1, count + 1)]
    largest = bound if full else min(bound, max(-(-total // count), total * portions[0] // sum(portions)))
    least = 1 if total - largest >= count - 1 else 0
    holding, surplus = [largest] + [least] * (count - 1), total - largest - least * (count - 1)
    while surplus > 0:
        movable = [i for i in range(1, count) if holding[i] < largest] or [i for i in range(1, count) if holding[i] < bound]
        whole, left = sum([portions[i] for i in movable]), surplus
        for i in movable:
            addition = min(bound - holding[i], max(1, left * portions[i] // whole), surplus)
            holding[i] = holding[i] + addition
            surplus = surplus - addition
    return np.array(holding)


def bell_draw(stream_key, shape, scale, most, shards=(), held_as=jnp.bfloat16):
    level = block_scale(stream_key, shape, shards, -0.22, 0.18) if shards else 1.0
    drawn = jax.random.normal(stream_key, shape, jnp.float32) * scale * level
    return jnp.minimum(jnp.maximum(drawn, -most), most).astype(held_as)


def heavy_noise(stream_key, shape, deviation, limit, shards, heavy, kind=jnp.bfloat16):
    entries = deviation * jax.random.normal(stream_key, shape, jnp.float32)
    if shards:
        entries = entries * block_scale(stream_key, shape, shards, -0.22, 0.18)
    return jnp.clip(strengthened(entries, jax.random.fold_in(stream_key, 3), *heavy), -limit, limit).astype(kind)


def setup_inputs(seed: int = 0, part: int = 0) -> dict:
    arg_keys = jax.random.split(jax.random.key(seed), 14)
    part_keys = jax.random.split(jax.random.fold_in(arg_keys[13], part), 14)
    tokens = bell_draw(part_keys[0], (TOKENS, D), 1.0, 6.0, ((0, 16),))
    cotangent = heavy_noise(part_keys[1], (TOKENS, D), 1.0, 6.0, ((0, 16),), (0, 1, 16, 2.0))
    route_ids_keys = jax.random.split(jax.random.fold_in(part_keys[2], 1), TOKENS // TOK_DEV)
    route_ids_turns = jax.random.permutation(jax.random.fold_in(part_keys[2], 3), TOKENS // TOK_DEV)
    route_ids = jax.vmap(lambda own, number: routed_block(jax.random.fold_in(part_keys[2], 2), own, number, TOK_DEV, EXPERTS, TOPK, CAP, 2))(route_ids_keys, route_ids_turns).reshape((TOKENS, TOPK))
    route_weights = jnp.clip(jnp.exp(math.log(1.0) - 2.9957323 * jax.random.uniform(part_keys[3], (TOKENS, TOPK), jnp.float32) ** block_scale(part_keys[3], (TOKENS, TOPK), ((0, 16),), -0.2, 0.2)), 0.05, 1.0)
    owner = jax.random.permutation(part_keys[4], EXPERTS).astype(jnp.int32)
    base_joined = bell_draw(arg_keys[5], (EXPERTS, D, 2 * FF), D ** -0.5, 0.125, ((0, 16),))
    base_down = bell_draw(arg_keys[6], (EXPERTS, FF, D), FF ** -0.5, 0.3125, ((0, 16),))
    master = bell_draw(part_keys[7], (EXPERTS, PFLAT), 0.05, 0.3, ((1, 16),), jnp.float32)
    moment = bell_draw(part_keys[8], (EXPERTS, PFLAT), 0.1, 0.6, ((1, 16),), jnp.float32)
    second = jnp.clip(jnp.exp(math.log(0.3) - 4.6051702 * jax.random.uniform(part_keys[9], (EXPERTS, PFLAT), jnp.float32) ** block_scale(part_keys[9], (EXPERTS, PFLAT), ((1, 16),), -0.2, 0.2)), 0.003, 0.3)
    step_rows = bell_draw(part_keys[10], (STEPS, DTOK, D), 1.0, 6.0, ((1, 16),))
    step_ids_keys = jax.random.split(jax.random.fold_in(part_keys[11], 1), STEPS * DTOK // DEC_DEV)
    step_ids_turns = jax.random.permutation(jax.random.fold_in(part_keys[11], 3), STEPS * DTOK // DEC_DEV)
    step_ids = jax.vmap(lambda own, number: routed_block(jax.random.fold_in(part_keys[11], 2), own, number, DEC_DEV, EXPERTS, TOPK, DCAP, 2))(step_ids_keys, step_ids_turns).reshape((STEPS, DTOK, TOPK))
    step_weights = jnp.clip(jnp.exp(math.log(1.0) - 2.9957323 * jax.random.uniform(part_keys[12], (STEPS, DTOK, TOPK), jnp.float32) ** block_scale(part_keys[12], (STEPS, DTOK, TOPK), ((1, 16),), -0.2, 0.2)), 0.05, 1.0)
    return dict(tokens=tokens, cotangent=cotangent, route_ids=route_ids, route_weights=route_weights, owner=owner, base_joined=base_joined, base_down=base_down, master=master, moment=moment, second=second, step_rows=step_rows, step_ids=step_ids, step_weights=step_weights)


adapter_scale_factor = 0.5
learn_rate = 0.05
beta_one = 0.9
beta_two = 0.999
decay_rate = 0.1
epsilon = 1e-08
bias_one = 1.0 - 0.9 ** 50
bias_two = 1.0 - 0.999 ** 50

def gated_product(left, right):
    return jnp.dot(left, right, preferred_element_type=jnp.float32)

def unpack(flat):
    cut_one = D * RANK
    cut_two = cut_one + RANK * 2 * FF
    cut_three = cut_two + FF * RANK
    a_in = flat[:cut_one].reshape(D, RANK)
    lowrank_input_factor = flat[cut_one:cut_two].reshape(RANK, 2 * FF)
    a_out = flat[cut_two:cut_three].reshape(FF, RANK)
    lowrank_output_factor = flat[cut_three:].reshape(RANK, D)
    return (a_in, lowrank_input_factor, a_out, lowrank_output_factor)

def expert_grads(token_rows_local, gradient_row_block, joined_weight, down_weight, flat_bf):
    a_in, lowrank_input_factor, a_out, lowrank_output_factor = unpack(flat_bf)
    middle_input_rows = gated_product(token_rows_local, a_in).astype(jnp.bfloat16)
    joined_projection = gated_product(token_rows_local, joined_weight) + adapter_scale_factor * gated_product(middle_input_rows, lowrank_input_factor)
    gate = joined_projection[:, :FF]
    up_part = joined_projection[:, FF:]
    sigma = jax.nn.sigmoid(gate)
    active = gate * sigma
    hidden_state = (active * up_part).astype(jnp.bfloat16)
    middle_output_rows = gated_product(hidden_state, a_out).astype(jnp.bfloat16)
    output_factor_gradient = adapter_scale_factor * gated_product(middle_output_rows.T, gradient_row_block)
    backward_middle_rows = (adapter_scale_factor * gated_product(gradient_row_block, lowrank_output_factor.T)).astype(jnp.bfloat16)
    grad_a_out = gated_product(hidden_state.T, backward_middle_rows)
    back_hidden = gated_product(gradient_row_block, down_weight.T) + gated_product(backward_middle_rows, a_out.T)
    back_gate = back_hidden * up_part * sigma * (1.0 + gate * (1.0 - sigma))
    back_up = back_hidden * active
    backward_joined_rows = jnp.concatenate([back_gate, back_up], axis=1).astype(jnp.bfloat16)
    input_factor_gradient = adapter_scale_factor * gated_product(middle_input_rows.T, backward_joined_rows)
    backward_input_rows = (adapter_scale_factor * gated_product(backward_joined_rows, lowrank_input_factor.T)).astype(jnp.bfloat16)
    grad_a_in = gated_product(token_rows_local.T, backward_input_rows)
    return jnp.concatenate([grad_a_in.reshape(-1), input_factor_gradient.reshape(-1), grad_a_out.reshape(-1), output_factor_gradient.reshape(-1)])

def expert_decode(token_rows_local, joined_weight, down_weight, flat_bf):
    a_in, lowrank_input_factor, a_out, lowrank_output_factor = unpack(flat_bf)
    middle_input_rows = gated_product(token_rows_local, a_in).astype(jnp.bfloat16)
    joined_projection = gated_product(token_rows_local, joined_weight) + adapter_scale_factor * gated_product(middle_input_rows, lowrank_input_factor)
    gate = joined_projection[:, :FF]
    hidden_state = (jax.nn.silu(gate) * joined_projection[:, FF:]).astype(jnp.bfloat16)
    middle_output_rows = gated_product(hidden_state, a_out).astype(jnp.bfloat16)
    return (gated_product(hidden_state, down_weight) + adapter_scale_factor * gated_product(middle_output_rows, lowrank_output_factor)).astype(jnp.bfloat16)

def adamw(master, moment, second, grads):
    moment_new = beta_one * moment + (1.0 - beta_one) * grads
    second_new = beta_two * second + (1.0 - beta_two) * grads * grads
    step_size = moment_new / bias_one / (jnp.sqrt(second_new / bias_two) + epsilon)
    return master - learn_rate * (step_size + decay_rate * master)

def slot_ranks(ids, block):
    token_rows_local = ids.shape[0]
    flat = ids.reshape(token_rows_local // block, block * TOPK)
    labels = jnp.arange(EXPERTS, dtype=jnp.int32)
    onehot = (flat[:, :, None] == labels[None, None, :]).astype(jnp.int32)
    before = jnp.cumsum(onehot, axis=1) - onehot
    return lax.optimization_barrier(jnp.sum(before * onehot, axis=2)).reshape(token_rows_local, TOPK)

def reference(tokens, cotangent, route_ids, route_weights, owner, base_joined, base_down, master, moment, second, step_rows, step_ids, step_weights):
    ranks = slot_ranks(route_ids, TOK_DEV)
    source = (jnp.arange(TOKENS, dtype=jnp.int32) // TOK_DEV)[:, None]
    slot_of = source * CAP + ranks
    cot_float = cotangent.astype(jnp.float32)

    def learn_one(expert):
        hit = route_ids == expert
        filled = jnp.any(hit, axis=1)
        slot = lax.optimization_barrier(jnp.sum(jnp.where(hit, slot_of, 0), axis=1)).astype(jnp.int32)
        weight = lax.optimization_barrier(jnp.sum(jnp.where(hit, route_weights, 0.0), axis=1))
        place = jnp.where(filled, slot, N_EP * CAP).astype(jnp.int32)
        token_rows_local = jnp.zeros((N_EP * CAP, D), jnp.bfloat16).at[place].set(tokens, mode='drop')
        scaled = (weight[:, None] * cot_float).astype(jnp.bfloat16)
        gradient_row_block = jnp.zeros((N_EP * CAP, D), jnp.bfloat16).at[place].set(scaled, mode='drop')
        held = owner[expert]
        return expert_grads(token_rows_local, gradient_row_block, base_joined[held], base_down[held], master[expert].astype(jnp.bfloat16))
    grads = lax.map(learn_one, jnp.arange(EXPERTS, dtype=jnp.int32))
    updated = adamw(master, moment, second, grads)
    fresh = updated.astype(jnp.bfloat16)
    dranks = slot_ranks(step_ids.reshape(STEPS * DTOK, TOPK), DEC_DEV).reshape(STEPS, DTOK, TOPK)
    dsource = (jnp.arange(DTOK, dtype=jnp.int32) // DEC_DEV)[:, None]
    dslot_of = dsource * DCAP + dranks

    def serve_one(total, expert):
        held = owner[expert]
        parts = []
        for step in range(STEPS):
            hit = step_ids[step] == expert
            filled = jnp.any(hit, axis=1)
            slot = lax.optimization_barrier(jnp.sum(jnp.where(hit, dslot_of[step], 0), axis=1)).astype(jnp.int32)
            weight = lax.optimization_barrier(jnp.sum(jnp.where(hit, step_weights[step], 0.0), axis=1))
            place = jnp.where(filled, slot, N_EP * DCAP).astype(jnp.int32)
            token_rows_local = jnp.zeros((N_EP * DCAP, D), jnp.bfloat16).at[place].set(step_rows[step], mode='drop')
            result = expert_decode(token_rows_local, base_joined[held], base_down[held], fresh[expert])
            picked = jnp.take(result, jnp.minimum(slot, N_EP * DCAP - 1), axis=0).astype(jnp.float32)
            parts.append(weight[:, None] * picked)
        return (total + jnp.stack(parts), None)
    total, _ = lax.scan(serve_one, jnp.zeros((STEPS, DTOK, D), jnp.float32), jnp.arange(EXPERTS, dtype=jnp.int32))
    return (updated, total.astype(jnp.bfloat16))
```

```python
import jax
import jax.numpy as jnp
from jax import lax
from jax.experimental import pallas as pl
from jax.experimental.pallas import tpu as pltpu
from jax.sharding import PartitionSpec as P

D = 2048
FF = 384
RANK = 32


adapter_scale_factor = 0.5
learn_rate = 0.05
beta_one = 0.9
beta_two = 0.999
decay_rate = 0.1
epsilon = 1e-08
bias_one = 1.0 - 0.9**50
bias_two = 1.0 - 0.999**50


def product(left, right):
    return jnp.dot(left, right, preferred_element_type=jnp.float32)


def unpack(flat):
    cut_one = D * RANK
    cut_two = cut_one + RANK * 2 * FF
    cut_three = cut_two + FF * RANK
    a_in = flat[:cut_one].reshape(D, RANK)
    b_in = flat[cut_one:cut_two].reshape(RANK, 2 * FF)
    a_out = flat[cut_two:cut_three].reshape(FF, RANK)
    b_out = flat[cut_three:].reshape(RANK, D)
    return (a_in, b_in, a_out, b_out)


def expert_grads(rows, grad_rows, joined_weight, down_weight, flat_bf):
    a_in, b_in, a_out, b_out = unpack(flat_bf)
    mid_in = product(rows, a_in).astype(jnp.bfloat16)
    joined = product(rows, joined_weight) + adapter_scale_factor * product(mid_in, b_in)
    gate = joined[:, :FF]
    up_part = joined[:, FF:]
    sigma = jax.nn.sigmoid(gate)
    active = gate * sigma
    hidden = (active * up_part).astype(jnp.bfloat16)
    mid_out = product(hidden, a_out).astype(jnp.bfloat16)
    grad_b_out = adapter_scale_factor * product(mid_out.T, grad_rows)
    back_mid = (adapter_scale_factor * product(grad_rows, b_out.T)).astype(jnp.bfloat16)
    grad_a_out = product(hidden.T, back_mid)
    back_hidden = product(grad_rows, down_weight.T) + product(back_mid, a_out.T)
    back_gate = back_hidden * up_part * sigma * (1.0 + gate * (1.0 - sigma))
    back_up = back_hidden * active
    back_joined = jnp.concatenate([back_gate, back_up], axis=1).astype(jnp.bfloat16)
    grad_b_in = adapter_scale_factor * product(mid_in.T, back_joined)
    back_in = (adapter_scale_factor * product(back_joined, b_in.T)).astype(jnp.bfloat16)
    grad_a_in = product(rows.T, back_in)
    return jnp.concatenate(
        [
            grad_a_in.reshape(-1),
            grad_b_in.reshape(-1),
            grad_a_out.reshape(-1),
            grad_b_out.reshape(-1),
        ]
    )


def train_kernel(
    tok,
    cot,
    weight,
    wf,
    wd,
    a_in,
    b_in,
    a_out,
    b_out,
    out_a_in,
    out_b_in,
    out_a_out,
    out_b_out,
    held_tok,
    held_cot,
    send,
    recv,
):
    devices = lax.axis_size("ep")
    chips = devices // 2
    half = chips // 2
    me = lax.axis_index("ep")
    core = lax.rem(me, 2)
    chip = me // 2
    place = jnp.where(lax.rem(chip, 2) == 0, chip // 2, chips - 1 - chip // 2)

    def chip_at(position):
        position = lax.rem(position + 2 * chips, chips)
        return jnp.where(position < half, 2 * position, 2 * (chips - 1 - position) + 1)

    right = 2 * chip_at(place + 1) + core
    left = 2 * chip_at(place - 1) + core
    sibling = 2 * chip + 1 - core
    held = (held_tok, held_cot)

    barrier = pltpu.get_barrier_semaphore()
    for other in (left, right, sibling):
        pl.semaphore_signal(
            barrier, inc=1, device_id={"ep": other}, device_id_type=pl.DeviceIdType.MESH
        )
    pl.semaphore_wait(barrier, 3)

    def move(kind, source, slot, other):
        return pltpu.make_async_remote_copy(
            src_ref=source,
            dst_ref=held[kind].at[slot],
            send_sem=send.at[kind, slot],
            recv_sem=recv.at[kind, slot],
            device_id={"ep": other},
            device_id_type=pl.DeviceIdType.MESH,
        )

    for kind, own in ((0, tok), (1, cot)):
        move(kind, own, 2, right).start()
        move(kind, own, 3, left).start()
        move(kind, own, 1, sibling).start()
    held_tok[0] = tok[...]
    held_cot[0] = cot[...]
    for out in (out_a_in, out_b_in, out_a_out, out_b_out):
        out[...] = jnp.zeros_like(out)

    def arrived(kind, slot):
        move(kind, held[kind].at[slot], slot, sibling).wait_recv()

    def outer(left_op, right_op):
        return lax.dot_general(
            left_op, right_op, (((0,), (0,)), ((), ())), preferred_element_type=jnp.float32
        )

    def times_transposed(left_op, right_op):
        return lax.dot_general(
            left_op, right_op, (((1,), (1,)), ((), ())), preferred_element_type=jnp.float32
        )

    def learn(tile, first, second):
        count, width = tok.shape
        pair = pl.ds(2 * tile, 2)
        rows = held_tok[pair].reshape(2 * count, width)
        gain = jnp.concatenate([weight[first], weight[second]], axis=0)
        grad = (gain * held_cot[pair].reshape(2 * count, width).astype(jnp.float32)).astype(
            jnp.bfloat16
        )
        mid_in = product(rows, a_in[...]).astype(jnp.bfloat16)
        joined = product(rows, wf[...]) + adapter_scale_factor * product(mid_in, b_in[...])
        gate = joined[:, :FF]
        up_part = joined[:, FF:]
        sigma = jax.nn.sigmoid(gate)
        active = gate * sigma
        hidden = (active * up_part).astype(jnp.bfloat16)
        mid_out = product(hidden, a_out[...]).astype(jnp.bfloat16)
        out_b_out[...] += adapter_scale_factor * outer(mid_out, grad)
        back_mid = (adapter_scale_factor * times_transposed(grad, b_out[...])).astype(jnp.bfloat16)
        out_a_out[...] += outer(back_mid, hidden)
        back_hidden = times_transposed(grad, wd[...]) + times_transposed(back_mid, a_out[...])
        back_gate = back_hidden * up_part * sigma * (1.0 + gate * (1.0 - sigma))
        back_up = back_hidden * active
        back_joined = jnp.concatenate([back_gate, back_up], axis=1).astype(jnp.bfloat16)
        out_b_in[...] += adapter_scale_factor * outer(mid_in, back_joined)
        back_in = (adapter_scale_factor * times_transposed(back_joined, b_in[...])).astype(
            jnp.bfloat16
        )
        out_a_in[...] += outer(back_in, rows)

    def step(s, carry):
        base = 4 * s - 2

        @pl.when(s == 0)
        def _():
            for kind in (0, 1):
                arrived(kind, 1)

        @pl.when((s > 0) & (s < half))
        def _():
            for kind in (0, 1):
                for way, onward in ((0, right), (1, left)):
                    slot = base + way
                    arrived(kind, slot)

                    @pl.when(s < half - 1)
                    def _():
                        move(kind, held[kind].at[slot], slot + 4, onward).start()

                    if way == kind:

                        @pl.when(s == half - 1)
                        def _():
                            move(kind, held[kind].at[slot], 4 * half - 2, onward).start()

                    move(kind, held[kind].at[slot], slot + 2, sibling).start()
            for kind in (0, 1):
                for way in (0, 1):
                    arrived(kind, base + 2 + way)

        @pl.when(s == half)
        def _():
            for kind in (0, 1):
                arrived(kind, base)
                move(kind, held[kind].at[base], base + 1, sibling).start()
            for kind in (0, 1):
                arrived(kind, base + 1)

        single = (s == 0) | (s == half)
        from_left = 2 * chip_at(place - s)
        from_right = 2 * chip_at(place + s)

        def tile_of(j, inner):
            which = core + j - 2 * core * j
            second = jnp.where(single, from_left + 1 - core, from_right + which)
            learn(jnp.where(s == 0, 0, 2 * s - 1) + j, from_left + which, second)
            return inner

        lax.fori_loop(0, jnp.where(single, 1, 2), tile_of, 0)
        return carry

    lax.fori_loop(0, half + 1, step, 0)

    def sent(slot, carry):
        for kind in (0, 1):
            move(kind, held[kind].at[slot], slot, sibling).wait_send()
        return carry

    lax.fori_loop(1, devices, sent, 0)


def train(tokens, cotangent, weight, joined_weight, down_weight, flat_bf):
    devices = lax.axis_size("ep")
    count, width = tokens.shape
    a_in, b_in, a_out, b_out = unpack(flat_bf)
    shape = lambda *size: jax.ShapeDtypeStruct(size, jnp.float32)
    vmem = pl.BlockSpec(memory_space=pltpu.VMEM)
    g_a_in, g_b_in, g_a_out, g_b_out = pl.pallas_call(
        train_kernel,
        out_shape=(shape(RANK, width), shape(RANK, 2 * FF), shape(RANK, FF), shape(RANK, width)),
        in_specs=[vmem] * 9,
        out_specs=(vmem,) * 4,
        scratch_shapes=[
            pltpu.VMEM((devices, count, width), jnp.bfloat16),
            pltpu.VMEM((devices, count, width), jnp.bfloat16),
            pltpu.SemaphoreType.DMA((2, devices)),
            pltpu.SemaphoreType.DMA((2, devices)),
        ],
        compiler_params=pltpu.CompilerParams(
            collective_id=0, has_side_effects=True, vmem_limit_bytes=56 * 1024 * 1024
        ),
        name="train",
    )(tokens, cotangent, weight, joined_weight, down_weight, a_in, b_in, a_out, b_out)
    return jnp.concatenate(
        [g_a_in.T.reshape(-1), g_b_in.reshape(-1), g_a_out.T.reshape(-1), g_b_out.reshape(-1)]
    )


def expert_decode(rows, joined_weight, down_weight, flat_bf):
    a_in, b_in, a_out, b_out = unpack(flat_bf)
    mid_in = product(rows, a_in).astype(jnp.bfloat16)
    joined = product(rows, joined_weight) + adapter_scale_factor * product(mid_in, b_in)
    gate = joined[:, :FF]
    hidden = (jax.nn.silu(gate) * joined[:, FF:]).astype(jnp.bfloat16)
    mid_out = product(hidden, a_out).astype(jnp.bfloat16)
    return (
        product(hidden, down_weight) + adapter_scale_factor * product(mid_out, b_out)
    ).astype(jnp.bfloat16)


def adamw(master, moment, second, grads):
    moment_new = beta_one * moment + (1.0 - beta_one) * grads
    second_new = beta_two * second + (1.0 - beta_two) * grads * grads
    step_size = moment_new / bias_one / (jnp.sqrt(second_new / bias_two) + epsilon)
    return master - learn_rate * (step_size + decay_rate * master)


def expert_weights(ids, weights, held_by):
    hit = ids[:, :, None] == held_by[None, None, :]
    return jnp.sum(jnp.where(hit, weights[:, :, None], 0.0), axis=1)


def exchange(array):
    return lax.all_to_all(array, "ep", split_axis=0, concat_axis=0, tiled=True)


def on_device(
    tokens,
    cotangent,
    route_ids,
    route_weights,
    owner,
    base_joined,
    base_down,
    master,
    moment,
    second,
    step_rows,
    step_ids,
    step_weights,
):
    experts = owner.shape[0]
    width = tokens.shape[1]
    me = lax.axis_index("ep")
    joined_weight = base_joined[0]
    down_weight = base_down[0]
    labels = jnp.arange(experts, dtype=jnp.int32)
    held_by = jnp.sum(jnp.where(owner[None, :] == labels[:, None], labels[None, :], 0), axis=1)
    steps, dec_rows = step_rows.shape[:2]

    def gather(array):
        return lax.all_gather(array, "ep", axis=0, tiled=True)

    my_weights = jnp.concatenate(
        [
            expert_weights(route_ids, route_weights, held_by),
            expert_weights(
                step_ids.reshape(steps * dec_rows, -1),
                step_weights.reshape(steps * dec_rows, -1),
                held_by,
            ),
        ]
    )
    all_weights = exchange(my_weights.T[:, None, :])[:, 0, :]
    tok_rows = tokens.shape[0]
    chunks = max(1, experts // 16)
    part = tok_rows // chunks
    flat_bf = exchange(jnp.take(master.astype(jnp.bfloat16), held_by, axis=0)).reshape(-1)
    all_steps = gather(step_rows.reshape(steps * dec_rows, width))
    if experts == 16:
        grads = train(
            tokens,
            cotangent,
            all_weights[:, :tok_rows, None],
            joined_weight,
            down_weight,
            flat_bf,
        )
    else:
        grads = 0.0
        for chunk in range(chunks):
            cut = slice(chunk * part, (chunk + 1) * part)
            all_tokens = gather(tokens[cut])
            all_cot = gather(cotangent[cut]).astype(jnp.float32)
            scaled = (all_weights[:, cut].reshape(-1, 1) * all_cot).astype(jnp.bfloat16)
            grads += expert_grads(all_tokens, scaled, joined_weight, down_weight, flat_bf)
    returned = exchange(grads.astype(jnp.bfloat16).reshape(experts, -1))
    my_grads = jnp.take(returned, owner, axis=0).astype(jnp.float32)
    updated = adamw(master, moment, second, my_grads)
    serving = exchange(jnp.take(updated.astype(jnp.bfloat16), held_by, axis=0)).reshape(-1)
    result = expert_decode(all_steps, joined_weight, down_weight, serving)
    back = exchange(result.reshape(experts, steps * dec_rows, width))
    mixed = jnp.sum(
        my_weights[tok_rows:].T[:, :, None] * back.astype(jnp.float32), axis=0
    )
    return (updated, mixed.astype(jnp.bfloat16).reshape(steps, dec_rows, width))


def solution(mesh):
    in_specs = (
        P(("grp", "ep"), None),
        P(("grp", "ep"), None),
        P(("grp", "ep"), None),
        P(("grp", "ep"), None),
        P("grp"),
        P("ep", None, None),
        P("ep", None, None),
        P("grp", "ep"),
        P("grp", "ep"),
        P("grp", "ep"),
        P(None, ("grp", "ep"), None),
        P(None, ("grp", "ep"), None),
        P(None, ("grp", "ep"), None),
    )
    out_specs = (P("grp", "ep"), P(None, ("grp", "ep"), None))
    return jax.shard_map(
        on_device, mesh=mesh, in_specs=in_specs, out_specs=out_specs, check_vma=False
    )
```

```python
import jax
import jax.numpy as jnp
from jax import lax
from jax.experimental import pallas as pl
from jax.experimental.pallas import tpu as pltpu
from jax.sharding import PartitionSpec as P

D = 2048
FF = 384
RANK = 32


adapter_scale_factor = 0.5
learn_rate = 0.05
beta_one = 0.9
beta_two = 0.999
decay_rate = 0.1
epsilon = 1e-08
bias_one = 1.0 - 0.9**50
bias_two = 1.0 - 0.999**50


def product(left, right):
    return jnp.dot(left, right, preferred_element_type=jnp.float32)


def unpack(flat):
    cut_one = D * RANK
    cut_two = cut_one + RANK * 2 * FF
    cut_three = cut_two + FF * RANK
    a_in = flat[:cut_one].reshape(D, RANK)
    b_in = flat[cut_one:cut_two].reshape(RANK, 2 * FF)
    a_out = flat[cut_two:cut_three].reshape(FF, RANK)
    b_out = flat[cut_three:].reshape(RANK, D)
    return (a_in, b_in, a_out, b_out)


def expert_grads(rows, grad_rows, joined_weight, down_weight, flat_bf):
    a_in, b_in, a_out, b_out = unpack(flat_bf)
    mid_in = product(rows, a_in).astype(jnp.bfloat16)
    joined = product(rows, joined_weight) + adapter_scale_factor * product(mid_in, b_in)
    gate = joined[:, :FF]
    up_part = joined[:, FF:]
    sigma = jax.nn.sigmoid(gate)
    active = gate * sigma
    hidden = (active * up_part).astype(jnp.bfloat16)
    mid_out = product(hidden, a_out).astype(jnp.bfloat16)
    grad_b_out = adapter_scale_factor * product(mid_out.T, grad_rows)
    back_mid = (adapter_scale_factor * product(grad_rows, b_out.T)).astype(jnp.bfloat16)
    grad_a_out = product(hidden.T, back_mid)
    back_hidden = product(grad_rows, down_weight.T) + product(back_mid, a_out.T)
    back_gate = back_hidden * up_part * sigma * (1.0 + gate * (1.0 - sigma))
    back_up = back_hidden * active
    back_joined = jnp.concatenate([back_gate, back_up], axis=1).astype(jnp.bfloat16)
    grad_b_in = adapter_scale_factor * product(mid_in.T, back_joined)
    back_in = (adapter_scale_factor * product(back_joined, b_in.T)).astype(jnp.bfloat16)
    grad_a_in = product(rows.T, back_in)
    return jnp.concatenate(
        [
            grad_a_in.reshape(-1),
            grad_b_in.reshape(-1),
            grad_a_out.reshape(-1),
            grad_b_out.reshape(-1),
        ]
    )


def train_kernel(
    tok,
    cot,
    weight,
    wf,
    wd,
    a_in,
    b_in,
    a_out,
    b_out,
    out_a_in,
    out_b_in,
    out_a_out,
    out_b_out,
    held_tok,
    held_cot,
    send,
    recv,
):
    devices = lax.axis_size("ep")
    chips = devices // 2
    half = chips // 2
    me = lax.axis_index("ep")
    core = lax.rem(me, 2)
    chip = me // 2
    place = jnp.where(lax.rem(chip, 2) == 0, chip // 2, chips - 1 - chip // 2)

    def chip_at(position):
        position = lax.rem(position + 2 * chips, chips)
        return jnp.where(position < half, 2 * position, 2 * (chips - 1 - position) + 1)

    right = 2 * chip_at(place + 1) + core
    left = 2 * chip_at(place - 1) + core
    sibling = 2 * chip + 1 - core
    held = (held_tok, held_cot)

    barrier = pltpu.get_barrier_semaphore()
    for other in (left, right, sibling):
        pl.semaphore_signal(
            barrier, inc=1, device_id={"ep": other}, device_id_type=pl.DeviceIdType.MESH
        )
    pl.semaphore_wait(barrier, 3)

    def move(kind, source, slot, other):
        return pltpu.make_async_remote_copy(
            src_ref=source,
            dst_ref=held[kind].at[slot],
            send_sem=send.at[kind, slot],
            recv_sem=recv.at[kind, slot],
            device_id={"ep": other},
            device_id_type=pl.DeviceIdType.MESH,
        )

    for kind, own in ((0, tok), (1, cot)):
        move(kind, own, 2, right).start()
        move(kind, own, 3, left).start()
        move(kind, own, 1, sibling).start()
    held_tok[0] = tok[...]
    held_cot[0] = cot[...]
    for out in (out_a_in, out_b_in, out_a_out, out_b_out):
        out[...] = jnp.zeros_like(out)

    def arrived(kind, slot):
        move(kind, held[kind].at[slot], slot, sibling).wait_recv()

    def outer(left_op, right_op):
        return lax.dot_general(
            left_op, right_op, (((0,), (0,)), ((), ())), preferred_element_type=jnp.float32
        )

    def times_transposed(left_op, right_op):
        return lax.dot_general(
            left_op, right_op, (((1,), (1,)), ((), ())), preferred_element_type=jnp.float32
        )

    def learn(tile, first, second):
        count, width = tok.shape
        pair = pl.ds(2 * tile, 2)
        rows = held_tok[pair].reshape(2 * count, width)
        gain = jnp.concatenate([weight[first], weight[second]], axis=0)
        grad = (gain * held_cot[pair].reshape(2 * count, width).astype(jnp.float32)).astype(
            jnp.bfloat16
        )
        mid_in = product(rows, a_in[...]).astype(jnp.bfloat16)
        joined = product(rows, wf[...]) + adapter_scale_factor * product(mid_in, b_in[...])
        gate = joined[:, :FF]
        up_part = joined[:, FF:]
        sigma = jax.nn.sigmoid(gate)
        active = gate * sigma
        hidden = (active * up_part).astype(jnp.bfloat16)
        mid_out = product(hidden, a_out[...]).astype(jnp.bfloat16)
        out_b_out[...] += adapter_scale_factor * outer(mid_out, grad)
        back_mid = (adapter_scale_factor * times_transposed(grad, b_out[...])).astype(jnp.bfloat16)
        out_a_out[...] += outer(back_mid, hidden)
        back_hidden = times_transposed(grad, wd[...]) + times_transposed(back_mid, a_out[...])
        back_gate = back_hidden * up_part * sigma * (1.0 + gate * (1.0 - sigma))
        back_up = back_hidden * active
        back_joined = jnp.concatenate([back_gate, back_up], axis=1).astype(jnp.bfloat16)
        out_b_in[...] += adapter_scale_factor * outer(mid_in, back_joined)
        back_in = (adapter_scale_factor * times_transposed(back_joined, b_in[...])).astype(
            jnp.bfloat16
        )
        out_a_in[...] += outer(back_in, rows)

    def step(s, carry):
        base = 4 * s - 2

        @pl.when(s == 0)
        def _():
            for kind in (0, 1):
                arrived(kind, 1)

        @pl.when((s > 0) & (s < half))
        def _():
            for kind in (0, 1):
                for way, onward in ((0, right), (1, left)):
                    slot = base + way
                    arrived(kind, slot)

                    @pl.when(s < half - 1)
                    def _():
                        move(kind, held[kind].at[slot], slot + 4, onward).start()

                    if way == kind:

                        @pl.when(s == half - 1)
                        def _():
                            move(kind, held[kind].at[slot], 4 * half - 2, onward).start()

                    move(kind, held[kind].at[slot], slot + 2, sibling).start()
            for kind in (0, 1):
                for way in (0, 1):
                    arrived(kind, base + 2 + way)

        @pl.when(s == half)
        def _():
            for kind in (0, 1):
                arrived(kind, base)
                move(kind, held[kind].at[base], base + 1, sibling).start()
            for kind in (0, 1):
                arrived(kind, base + 1)

        single = (s == 0) | (s == half)
        from_left = 2 * chip_at(place - s)
        from_right = 2 * chip_at(place + s)

        def tile_of(j, inner):
            which = core + j - 2 * core * j
            second = jnp.where(single, from_left + 1 - core, from_right + which)
            learn(jnp.where(s == 0, 0, 2 * s - 1) + j, from_left + which, second)
            return inner

        lax.fori_loop(0, jnp.where(single, 1, 2), tile_of, 0)
        return carry

    lax.fori_loop(0, half + 1, step, 0)

    def sent(slot, carry):
        for kind in (0, 1):
            move(kind, held[kind].at[slot], slot, sibling).wait_send()
        return carry

    lax.fori_loop(1, devices, sent, 0)


def train(tokens, cotangent, weight, joined_weight, down_weight, flat_bf):
    devices = lax.axis_size("ep")
    count, width = tokens.shape
    a_in, b_in, a_out, b_out = unpack(flat_bf)
    shape = lambda *size: jax.ShapeDtypeStruct(size, jnp.float32)
    vmem = pl.BlockSpec(memory_space=pltpu.VMEM)
    g_a_in, g_b_in, g_a_out, g_b_out = pl.pallas_call(
        train_kernel,
        out_shape=(shape(RANK, width), shape(RANK, 2 * FF), shape(RANK, FF), shape(RANK, width)),
        in_specs=[vmem] * 9,
        out_specs=(vmem,) * 4,
        scratch_shapes=[
            pltpu.VMEM((devices, count, width), jnp.bfloat16),
            pltpu.VMEM((devices, count, width), jnp.bfloat16),
            pltpu.SemaphoreType.DMA((2, devices)),
            pltpu.SemaphoreType.DMA((2, devices)),
        ],
        compiler_params=pltpu.CompilerParams(
            collective_id=0, has_side_effects=True, vmem_limit_bytes=56 * 1024 * 1024
        ),
        name="train",
    )(tokens, cotangent, weight, joined_weight, down_weight, a_in, b_in, a_out, b_out)
    return jnp.concatenate(
        [g_a_in.T.reshape(-1), g_b_in.reshape(-1), g_a_out.T.reshape(-1), g_b_out.reshape(-1)]
    )


def snake(devices):
    chips = devices // 2
    half = chips // 2
    me = lax.axis_index("ep")
    core = lax.rem(me, 2)
    chip = me // 2
    place = jnp.where(lax.rem(chip, 2) == 0, chip // 2, chips - 1 - chip // 2)

    def chip_at(position):
        position = lax.rem(position + 2 * chips, chips)
        return jnp.where(position < half, 2 * position, 2 * (chips - 1 - position) + 1)

    return me, core, chip, place, chip_at


def spread(block):
    pieces = []
    for start in range(0, block.shape[0], 128):
        cut = block[start : start + 128]
        count = cut.shape[0]
        shape = (4 * count, count)
        rows = lax.broadcasted_iota(jnp.int32, shape, 0)
        repeat = (rows // 4 == lax.broadcasted_iota(jnp.int32, shape, 1)).astype(jnp.bfloat16)
        wide = product(repeat, cut)
        shape = (4 * count, 128)
        rows = lax.broadcasted_iota(jnp.int32, shape, 0)
        lanes = lax.broadcasted_iota(jnp.int32, shape, 1)
        wide = jnp.where(lanes // RANK == lax.rem(rows, 4), wide, 0.0).astype(jnp.bfloat16)
        shape = (128, RANK)
        lanes = lax.broadcasted_iota(jnp.int32, shape, 0)
        fold = (lax.rem(lanes, RANK) == lax.broadcasted_iota(jnp.int32, shape, 1)).astype(
            jnp.bfloat16
        )
        pieces.append(product(wide, fold).astype(jnp.bfloat16))
    return jnp.concatenate(pieces, axis=0)


def weave(block):
    count = block.shape[0]
    times = count // RANK
    shape = (count, count)
    rows = lax.broadcasted_iota(jnp.int32, shape, 0)
    source = lax.rem(rows, RANK) * times + rows // RANK
    pick = (source == lax.broadcasted_iota(jnp.int32, shape, 1)).astype(jnp.bfloat16)
    sorted_rows = product(pick, block).astype(jnp.bfloat16)
    return jnp.concatenate(
        [sorted_rows[RANK * j : RANK * (j + 1)] for j in range(times)], axis=1
    )


def restore(pieces, flat, factors):
    count = pieces.shape[1]
    for j in range(pieces.shape[0]):
        flat[count * j : count * (j + 1), :] = pieces[j].astype(jnp.float32)
    cuts = [0]
    for size in (D * RANK, RANK * 2 * FF, FF * RANK, RANK * D):
        cuts.append(cuts[-1] + size // 128)
    for k, undo in enumerate((spread, weave, spread, weave)):
        factors[k][...] = undo(flat[cuts[k] : cuts[k + 1], :].astype(jnp.bfloat16))


def serve_kernel(
    owner,
    held_by,
    grads,
    master,
    moment,
    second,
    rows_in,
    weight,
    wf,
    wd,
    updated,
    decoded,
    got_grads,
    fresh,
    serving,
    pieces,
    flat,
    a_in,
    b_in,
    a_out,
    b_out,
    held,
    base,
    keep,
    give,
    got,
    out_buf,
    in_buf,
    piece_send,
    piece_recv,
    row_send,
    row_recv,
    give_send,
    give_recv,
    sum_send,
    sum_recv,
):
    devices = lax.axis_size("ep")
    half = devices // 4
    me, core, chip, place, chip_at = snake(devices)
    right = 2 * chip_at(place + 1) + core
    left = 2 * chip_at(place - 1) + core
    sibling = 2 * chip + 1 - core
    count = rows_in.shape[0]
    part = count // 2

    barrier = pltpu.get_barrier_semaphore()

    def greet(k, carry):
        pl.semaphore_signal(
            barrier,
            inc=1,
            device_id={"ep": lax.rem(me + k, devices)},
            device_id_type=pl.DeviceIdType.MESH,
        )
        return carry

    lax.fori_loop(1, devices, greet, 0)
    pl.semaphore_wait(barrier, devices - 1)

    def remote(source, target, send, recv, other):
        return pltpu.make_async_remote_copy(
            src_ref=source,
            dst_ref=target,
            send_sem=send,
            recv_sem=recv,
            device_id={"ep": other},
            device_id_type=pl.DeviceIdType.MESH,
        )

    def piece_to(kind, source, target, other):
        return remote(
            source.at[other],
            target.at[me],
            piece_send.at[kind, other],
            piece_recv.at[kind, me],
            other,
        )

    def piece_from(kind, source, target, other):
        return remote(
            source.at[other],
            target.at[other],
            piece_send.at[kind, other],
            piece_recv.at[kind, other],
            other,
        )

    def each_other(act):
        def body(k, carry):
            act(lax.rem(me + k, devices))
            return carry

        lax.fori_loop(1, devices, body, 0)

    each_other(lambda other: piece_to(0, grads, got_grads, other).start())

    def cut(slot, kind):
        return held.at[slot, pl.ds(part * kind, part)]

    def row_move(source, slot, kind, other):
        return remote(
            source, cut(slot, kind), row_send.at[kind, slot], row_recv.at[kind, slot], other
        )

    def row_arrived(slot, kind):
        row_move(cut(slot, kind), slot, kind, sibling).wait_recv()

    for kind in (0, 1):
        own = rows_in.at[pl.ds(part * kind, part)]
        row_move(own, 4, kind, right).start()
        row_move(own, 5, kind, left).start()
        row_move(own, 2, kind, sibling).start()
    held[0] = rows_in[...]
    got_grads[me] = grads[me]
    each_other(lambda other: piece_from(0, grads, got_grads, other).wait_recv())

    def renew(k, carry):
        other = lax.rem(me + k, devices)
        expert = held_by[other]
        fresh[other] = adamw(
            master[expert], moment[expert], second[expert], got_grads[other].astype(jnp.float32)
        )
        serving[other] = fresh[other].astype(jnp.bfloat16)

        @pl.when(k < devices)
        def _():
            piece_to(1, serving, pieces, other).start()

        return carry

    lax.fori_loop(1, devices + 1, renew, 0)
    pieces[me] = serving[me]

    def row_step(s, carry):
        for kind in (0, 1):
            for way, onward in ((0, right), (1, left)):
                slot = 4 * s + way
                row_arrived(slot, kind)

                @pl.when(s < half - 1)
                def _():
                    row_move(cut(slot, kind), slot + 4, kind, onward).start()

                if way == kind:

                    @pl.when(s == half - 1)
                    def _():
                        row_move(cut(slot, kind), 1, kind, onward).start()

                row_move(cut(slot, kind), slot + 2, kind, sibling).start()
        return carry

    lax.fori_loop(1, half, row_step, 0)

    def write_back(expert, carry):
        updated[expert] = fresh[owner[expert]]
        return carry

    lax.fori_loop(0, devices, write_back, 0)
    for kind in (0, 1):
        row_arrived(1, kind)
        row_move(cut(1, kind), 3, kind, sibling).start()

    def rest(slot, carry):
        for kind in (0, 1):
            row_arrived(slot, kind)
        return carry

    lax.fori_loop(2, 4, rest, 0)
    for s in range(1, half):
        lax.fori_loop(4 * s + 2, 4 * s + 4, rest, 0)

    def base_of(tile, carry):
        rows = held[pl.ds(8 * tile, 8)].reshape(8 * count, rows_in.shape[1])
        base[tile] = product(rows, wf[...])
        return carry

    lax.fori_loop(0, devices // 8, base_of, 0)
    each_other(lambda other: piece_from(1, serving, pieces, other).wait_recv())
    restore(pieces, flat, (a_in, b_in, a_out, b_out))

    def answer(k, carry):
        s = jnp.where(k == 0, 0, half - k)
        rows = held[pl.ds(4 * s, 4)].reshape(4 * count, rows_in.shape[1])
        mid_in = product(rows, a_in[...]).astype(jnp.bfloat16)
        from_base = base[s // 2, pl.ds(lax.rem(s, 2) * 4 * count, 4 * count), :]
        joined = from_base + adapter_scale_factor * product(mid_in, b_in[...])
        gate = joined[:, :FF]
        hidden = (gate * jax.nn.sigmoid(gate) * joined[:, FF:]).astype(jnp.bfloat16)
        mid_out = product(hidden, a_out[...]).astype(jnp.bfloat16)
        result = product(hidden, wd[...]) + adapter_scale_factor * product(mid_out, b_out[...])
        result = result.astype(jnp.bfloat16).astype(jnp.float32)
        first = 2 * chip_at(place - s)
        second_chip = 2 * chip_at(place + jnp.where(s == 0, half, s))
        gains = jnp.concatenate(
            [
                weight[first + core],
                weight[second_chip + core],
                weight[first + 1 - core],
                weight[second_chip + 1 - core],
            ],
            axis=0,
        )
        result = (gains * result).reshape(4, count, rows_in.shape[1])
        keep[s] = result[:2]
        give[s] = result[2:].astype(jnp.bfloat16)
        remote(give.at[s], got.at[s], give_send.at[s], give_recv.at[s], sibling).start()
        return carry

    lax.fori_loop(0, half, answer, 0)

    def sum_move(way, t, piece, other):
        spot = pl.ds(part * piece, part)
        return remote(
            out_buf.at[way, t, spot],
            in_buf.at[way, t, spot],
            sum_send.at[way, t, piece],
            sum_recv.at[way, t, piece],
            other,
        )

    def got_wait(s):
        remote(give.at[s], got.at[s], give_send.at[s], give_recv.at[s], sibling).wait_recv()

    def of_chip(s, way):
        return keep[s, way] + got[s, way].astype(jnp.float32)

    got_wait(0)
    opposite = of_chip(0, 1).astype(jnp.bfloat16)
    for way, onward in ((0, right), (1, left)):
        out_buf[way, 0, part * way : part * (way + 1), :] = opposite[part * way : part * (way + 1)]
        sum_move(way, 0, way, onward).start()
    for t in range(1, half):
        s = half - t
        got_wait(s)
        for way, onward in ((0, right), (1, left)):
            total = of_chip(s, 1 - way)
            for piece in (0, 1):
                low, high = part * piece, part * (piece + 1)
                term = total[low:high]
                if t > 1 or piece == way:
                    sum_move(way, t - 1, piece, onward).wait_recv()
                    term = term + in_buf[way, t - 1, low:high, :].astype(jnp.float32)
                out_buf[way, t, low:high, :] = term.astype(jnp.bfloat16)
                sum_move(way, t, piece, onward).start()
    total = of_chip(0, 0)
    for way in (0, 1):
        for piece in (0, 1):
            sum_move(way, half - 1, piece, left).wait_recv()
        total = total + in_buf[way, half - 1].astype(jnp.float32)
    decoded[...] = total.astype(jnp.bfloat16)

    def piece_sent(other):
        piece_to(0, grads, got_grads, other).wait_send()
        piece_to(1, serving, pieces, other).wait_send()

    each_other(piece_sent)

    def rows_sent(slot, carry):
        for kind in (0, 1):
            row_move(cut(slot, kind), slot, kind, sibling).wait_send()
        return carry

    lax.fori_loop(1, devices, rows_sent, 0)
    for s in range(half):
        remote(give.at[s], got.at[s], give_send.at[s], give_recv.at[s], sibling).wait_send()
    for way in (0, 1):
        for t in range(half):
            for piece in (0, 1):
                if t > 0 or piece == way:
                    sum_move(way, t, piece, left).wait_send()


def serve(owner, held_by, grads, master, moment, second, rows, weight, joined_weight, down_weight):
    devices = lax.axis_size("ep")
    half = devices // 4
    count, width = rows.shape
    lane_rows = master.shape[1] // 128
    cube = (devices, lane_rows, 128)
    vmem = pl.BlockSpec(memory_space=pltpu.VMEM)
    smem = pl.BlockSpec(memory_space=pltpu.SMEM)
    bf, f32 = jnp.bfloat16, jnp.float32
    updated, decoded = pl.pallas_call(
        serve_kernel,
        out_shape=(jax.ShapeDtypeStruct(cube, f32), jax.ShapeDtypeStruct((count, width), bf)),
        in_specs=[smem] * 2 + [vmem] * 8,
        out_specs=(vmem,) * 2,
        scratch_shapes=[
            pltpu.VMEM(cube, bf),
            pltpu.VMEM(cube, f32),
            pltpu.VMEM(cube, bf),
            pltpu.VMEM(cube, bf),
            pltpu.VMEM((devices * lane_rows, 128), f32),
            pltpu.VMEM((width, RANK), bf),
            pltpu.VMEM((RANK, 2 * FF), bf),
            pltpu.VMEM((FF, RANK), bf),
            pltpu.VMEM((RANK, width), bf),
            pltpu.VMEM((devices, count, width), bf),
            pltpu.VMEM((devices // 8, 8 * count, 2 * FF), f32),
            pltpu.VMEM((half, 2, count, width), f32),
            pltpu.VMEM((half, 2, count, width), bf),
            pltpu.VMEM((half, 2, count, width), bf),
            pltpu.VMEM((2, half, count, width), bf),
            pltpu.VMEM((2, half, count, width), bf),
            pltpu.SemaphoreType.DMA((2, devices)),
            pltpu.SemaphoreType.DMA((2, devices)),
            pltpu.SemaphoreType.DMA((2, devices)),
            pltpu.SemaphoreType.DMA((2, devices)),
            pltpu.SemaphoreType.DMA((half,)),
            pltpu.SemaphoreType.DMA((half,)),
            pltpu.SemaphoreType.DMA((2, half, 2)),
            pltpu.SemaphoreType.DMA((2, half, 2)),
        ],
        compiler_params=pltpu.CompilerParams(
            collective_id=1, has_side_effects=True, vmem_limit_bytes=56 * 1024 * 1024
        ),
        name="serve",
    )(
        owner,
        held_by,
        grads.astype(bf).reshape(cube),
        master.reshape(cube),
        moment.reshape(cube),
        second.reshape(cube),
        rows,
        weight,
        joined_weight,
        down_weight,
    )
    return updated.reshape(master.shape), decoded


def expert_decode(rows, joined_weight, down_weight, flat_bf):
    a_in, b_in, a_out, b_out = unpack(flat_bf)
    mid_in = product(rows, a_in).astype(jnp.bfloat16)
    joined = product(rows, joined_weight) + adapter_scale_factor * product(mid_in, b_in)
    gate = joined[:, :FF]
    hidden = (jax.nn.silu(gate) * joined[:, FF:]).astype(jnp.bfloat16)
    mid_out = product(hidden, a_out).astype(jnp.bfloat16)
    return (
        product(hidden, down_weight) + adapter_scale_factor * product(mid_out, b_out)
    ).astype(jnp.bfloat16)


def adamw(master, moment, second, grads):
    moment_new = beta_one * moment + (1.0 - beta_one) * grads
    second_new = beta_two * second + (1.0 - beta_two) * grads * grads
    step_size = moment_new / bias_one / (jnp.sqrt(second_new / bias_two) + epsilon)
    return master - learn_rate * (step_size + decay_rate * master)


def expert_weights(ids, weights, held_by):
    hit = ids[:, :, None] == held_by[None, None, :]
    return jnp.sum(jnp.where(hit, weights[:, :, None], 0.0), axis=1)


def exchange(array):
    return lax.all_to_all(array, "ep", split_axis=0, concat_axis=0, tiled=True)


def on_device(
    tokens,
    cotangent,
    route_ids,
    route_weights,
    owner,
    base_joined,
    base_down,
    master,
    moment,
    second,
    step_rows,
    step_ids,
    step_weights,
):
    experts = owner.shape[0]
    width = tokens.shape[1]
    me = lax.axis_index("ep")
    joined_weight = base_joined[0]
    down_weight = base_down[0]
    labels = jnp.arange(experts, dtype=jnp.int32)
    held_by = jnp.sum(jnp.where(owner[None, :] == labels[:, None], labels[None, :], 0), axis=1)
    steps, dec_rows = step_rows.shape[:2]

    def gather(array):
        return lax.all_gather(array, "ep", axis=0, tiled=True)

    my_weights = jnp.concatenate(
        [
            expert_weights(route_ids, route_weights, held_by),
            expert_weights(
                step_ids.reshape(steps * dec_rows, -1),
                step_weights.reshape(steps * dec_rows, -1),
                held_by,
            ),
        ]
    )
    all_weights = exchange(my_weights.T[:, None, :])[:, 0, :]
    tok_rows = tokens.shape[0]
    chunks = max(1, experts // 16)
    part = tok_rows // chunks
    flat_bf = exchange(jnp.take(master.astype(jnp.bfloat16), held_by, axis=0)).reshape(-1)
    if experts == 16:
        grads = train(
            tokens,
            cotangent,
            all_weights[:, :tok_rows, None],
            joined_weight,
            down_weight,
            flat_bf,
        )
        updated, decoded = serve(
            owner,
            held_by,
            grads,
            master,
            moment,
            second,
            step_rows.reshape(steps * dec_rows, width),
            all_weights[:, tok_rows:, None],
            joined_weight,
            down_weight,
        )
        return (updated, decoded.reshape(steps, dec_rows, width))
    grads = 0.0
    for chunk in range(chunks):
        cut = slice(chunk * part, (chunk + 1) * part)
        all_tokens = gather(tokens[cut])
        all_cot = gather(cotangent[cut]).astype(jnp.float32)
        scaled = (all_weights[:, cut].reshape(-1, 1) * all_cot).astype(jnp.bfloat16)
        grads += expert_grads(all_tokens, scaled, joined_weight, down_weight, flat_bf)
    all_steps = gather(step_rows.reshape(steps * dec_rows, width))
    returned = exchange(grads.astype(jnp.bfloat16).reshape(experts, -1))
    my_grads = jnp.take(returned, owner, axis=0).astype(jnp.float32)
    updated = adamw(master, moment, second, my_grads)
    serving = exchange(jnp.take(updated.astype(jnp.bfloat16), held_by, axis=0)).reshape(-1)
    result = expert_decode(all_steps, joined_weight, down_weight, serving)
    back = exchange(result.reshape(experts, steps * dec_rows, width))
    mixed = jnp.sum(
        my_weights[tok_rows:].T[:, :, None] * back.astype(jnp.float32), axis=0
    )
    return (updated, mixed.astype(jnp.bfloat16).reshape(steps, dec_rows, width))


def solution(mesh):
    in_specs = (
        P(("grp", "ep"), None),
        P(("grp", "ep"), None),
        P(("grp", "ep"), None),
        P(("grp", "ep"), None),
        P("grp"),
        P("ep", None, None),
        P("ep", None, None),
        P("grp", "ep"),
        P("grp", "ep"),
        P("grp", "ep"),
        P(None, ("grp", "ep"), None),
        P(None, ("grp", "ep"), None),
        P(None, ("grp", "ep"), None),
    )
    out_specs = (P("grp", "ep"), P(None, ("grp", "ep"), None))
    return jax.shard_map(
        on_device, mesh=mesh, in_specs=in_specs, out_specs=out_specs, check_vma=False
    )
```

```python
import jax
import jax.numpy as jnp
from jax import lax
from jax.experimental import pallas as pl
from jax.experimental.pallas import tpu as pltpu
from jax.sharding import PartitionSpec as P

D = 2048
FF = 384
RANK = 32


adapter_scale_factor = 0.5
learn_rate = 0.05
beta_one = 0.9
beta_two = 0.999
decay_rate = 0.1
epsilon = 1e-08
bias_one = 1.0 - 0.9**50
bias_two = 1.0 - 0.999**50


def product(left, right):
    return jnp.dot(left, right, preferred_element_type=jnp.float32)


def unpack(flat):
    cut_one = D * RANK
    cut_two = cut_one + RANK * 2 * FF
    cut_three = cut_two + FF * RANK
    a_in = flat[:cut_one].reshape(D, RANK)
    b_in = flat[cut_one:cut_two].reshape(RANK, 2 * FF)
    a_out = flat[cut_two:cut_three].reshape(FF, RANK)
    b_out = flat[cut_three:].reshape(RANK, D)
    return (a_in, b_in, a_out, b_out)


def expert_grads(rows, grad_rows, joined_weight, down_weight, flat_bf):
    a_in, b_in, a_out, b_out = unpack(flat_bf)
    mid_in = product(rows, a_in).astype(jnp.bfloat16)
    joined = product(rows, joined_weight) + adapter_scale_factor * product(mid_in, b_in)
    gate = joined[:, :FF]
    up_part = joined[:, FF:]
    sigma = jax.nn.sigmoid(gate)
    active = gate * sigma
    hidden = (active * up_part).astype(jnp.bfloat16)
    mid_out = product(hidden, a_out).astype(jnp.bfloat16)
    grad_b_out = adapter_scale_factor * product(mid_out.T, grad_rows)
    back_mid = (adapter_scale_factor * product(grad_rows, b_out.T)).astype(jnp.bfloat16)
    grad_a_out = product(hidden.T, back_mid)
    back_hidden = product(grad_rows, down_weight.T) + product(back_mid, a_out.T)
    back_gate = back_hidden * up_part * sigma * (1.0 + gate * (1.0 - sigma))
    back_up = back_hidden * active
    back_joined = jnp.concatenate([back_gate, back_up], axis=1).astype(jnp.bfloat16)
    grad_b_in = adapter_scale_factor * product(mid_in.T, back_joined)
    back_in = (adapter_scale_factor * product(back_joined, b_in.T)).astype(jnp.bfloat16)
    grad_a_in = product(rows.T, back_in)
    return jnp.concatenate(
        [
            grad_a_in.reshape(-1),
            grad_b_in.reshape(-1),
            grad_a_out.reshape(-1),
            grad_b_out.reshape(-1),
        ]
    )


def snake(devices):
    chips = devices // 2
    half = chips // 2
    me = lax.axis_index("ep")
    core = lax.rem(me, 2)
    chip = me // 2
    place = jnp.where(lax.rem(chip, 2) == 0, chip // 2, chips - 1 - chip // 2)

    def chip_at(position):
        position = lax.rem(position + 2 * chips, chips)
        return jnp.where(position < half, 2 * position, 2 * (chips - 1 - position) + 1)

    return me, core, chip, place, chip_at


def spread(block):
    pieces = []
    for start in range(0, block.shape[0], 128):
        cut = block[start : start + 128]
        count = cut.shape[0]
        shape = (4 * count, count)
        rows = lax.broadcasted_iota(jnp.int32, shape, 0)
        repeat = (rows // 4 == lax.broadcasted_iota(jnp.int32, shape, 1)).astype(jnp.bfloat16)
        wide = product(repeat, cut)
        shape = (4 * count, 128)
        rows = lax.broadcasted_iota(jnp.int32, shape, 0)
        lanes = lax.broadcasted_iota(jnp.int32, shape, 1)
        wide = jnp.where(lanes // RANK == lax.rem(rows, 4), wide, 0.0).astype(jnp.bfloat16)
        shape = (128, RANK)
        lanes = lax.broadcasted_iota(jnp.int32, shape, 0)
        fold = (lax.rem(lanes, RANK) == lax.broadcasted_iota(jnp.int32, shape, 1)).astype(
            jnp.bfloat16
        )
        pieces.append(product(wide, fold).astype(jnp.bfloat16))
    return jnp.concatenate(pieces, axis=0)


def weave(block):
    count = block.shape[0]
    times = count // RANK
    shape = (count, count)
    rows = lax.broadcasted_iota(jnp.int32, shape, 0)
    source = lax.rem(rows, RANK) * times + rows // RANK
    pick = (source == lax.broadcasted_iota(jnp.int32, shape, 1)).astype(jnp.bfloat16)
    sorted_rows = product(pick, block).astype(jnp.bfloat16)
    return jnp.concatenate(
        [sorted_rows[RANK * j : RANK * (j + 1)] for j in range(times)], axis=1
    )


def unspread(block):
    pieces = []
    for start in range(0, block.shape[1], 512):
        cut = block[:, start : start + 512]
        count = cut.shape[1]
        shape = (RANK, 128)
        rows = lax.broadcasted_iota(jnp.int32, shape, 0)
        lanes = lax.broadcasted_iota(jnp.int32, shape, 1)
        tile = (lax.rem(lanes, RANK) == rows).astype(jnp.bfloat16)
        wide = outer(cut, tile)
        shape = (count, 128)
        rows = lax.broadcasted_iota(jnp.int32, shape, 0)
        lanes = lax.broadcasted_iota(jnp.int32, shape, 1)
        wide = jnp.where(lanes // RANK == lax.rem(rows, 4), wide, 0.0).astype(jnp.bfloat16)
        shape = (count // 4, count)
        rows = lax.broadcasted_iota(jnp.int32, shape, 0)
        collapse = (rows == lax.broadcasted_iota(jnp.int32, shape, 1) // 4).astype(jnp.bfloat16)
        pieces.append(product(collapse, wide))
    return jnp.concatenate(pieces, axis=0)


def unweave(block):
    times = block.shape[1] // 128
    stacked = jnp.concatenate([block[:, 128 * j : 128 * (j + 1)] for j in range(times)], axis=0)
    shape = (RANK * times, RANK * times)
    rows = lax.broadcasted_iota(jnp.int32, shape, 0)
    source = lax.rem(rows, times) * RANK + rows // times
    pick = (source == lax.broadcasted_iota(jnp.int32, shape, 1)).astype(jnp.bfloat16)
    return product(pick, stacked)


def flatten(gradients, flat, pieces):
    start = 0
    for grad, undo in zip(gradients, (unspread, unweave, unspread, unweave)):
        rows = undo(grad[...].astype(jnp.bfloat16))
        flat[start : start + rows.shape[0], :] = rows
        start += rows.shape[0]
    count = pieces.shape[1]
    for j in range(pieces.shape[0]):
        pieces[j] = flat[count * j : count * (j + 1), :].astype(jnp.bfloat16)


def outer(left_op, right_op):
    return lax.dot_general(
        left_op, right_op, (((0,), (0,)), ((), ())), preferred_element_type=jnp.float32
    )


def times_transposed(left_op, right_op):
    return lax.dot_general(
        left_op, right_op, (((1,), (1,)), ((), ())), preferred_element_type=jnp.float32
    )


def column(row):
    shape = (row.shape[1], row.shape[1])
    same = lax.broadcasted_iota(jnp.int32, shape, 0) == lax.broadcasted_iota(jnp.int32, shape, 1)
    return jnp.sum(jnp.where(same, row, 0.0), axis=1, keepdims=True)


def restore(pieces, flat, factors):
    count = pieces.shape[1]
    for j in range(pieces.shape[0]):
        flat[count * j : count * (j + 1), :] = pieces[j].astype(jnp.float32)
    cuts = [0]
    for size in (D * RANK, RANK * 2 * FF, FF * RANK, RANK * D):
        cuts.append(cuts[-1] + size // 128)
    for k, undo in enumerate((spread, weave, spread, weave)):
        factors[k][...] = undo(flat[cuts[k] : cuts[k + 1], :].astype(jnp.bfloat16))


def job_kernel(
    owner,
    held_by,
    tok,
    cot,
    ids,
    gains_in,
    rows_in,
    master,
    moment_in,
    second_in,
    wf_in,
    wd_in,
    updated,
    decoded,
    wf,
    wd,
    moment,
    second,
    held_tok,
    held_cot,
    sent_gain,
    gain,
    sent_master,
    got_master,
    grads,
    out_a_in,
    out_b_in,
    out_a_out,
    out_b_out,
    got_grads,
    fresh,
    serving,
    pieces,
    flat,
    a_in,
    b_in,
    a_out,
    b_out,
    held,
    base,
    keep,
    give,
    got,
    out_buf,
    in_buf,
    load_sem,
    big_send,
    big_recv,
    gain_send,
    gain_recv,
    piece_send,
    piece_recv,
    row_send,
    row_recv,
    give_send,
    give_recv,
    sum_send,
    sum_recv,
):
    devices = lax.axis_size("ep")
    half = devices // 4
    me, core, chip, place, chip_at = snake(devices)
    right = 2 * chip_at(place + 1) + core
    left = 2 * chip_at(place - 1) + core
    sibling = 2 * chip + 1 - core
    count = rows_in.shape[0]
    part = count // 2

    loads = [
        pltpu.make_async_copy(source, target, load_sem.at[k])
        for k, (source, target) in enumerate(
            ((wf_in, wf), (wd_in, wd), (moment_in, moment), (second_in, second))
        )
    ]
    for load in loads:
        load.start()
    bigs = (held_tok, held_cot)
    barrier = pltpu.get_barrier_semaphore()

    def greet(k, carry):
        pl.semaphore_signal(
            barrier,
            inc=1,
            device_id={"ep": lax.rem(me + k, devices)},
            device_id_type=pl.DeviceIdType.MESH,
        )
        return carry

    lax.fori_loop(1, devices, greet, 0)
    pl.semaphore_wait(barrier, devices - 1)

    def remote(source, target, send, recv, other):
        return pltpu.make_async_remote_copy(
            src_ref=source,
            dst_ref=target,
            send_sem=send,
            recv_sem=recv,
            device_id={"ep": other},
            device_id_type=pl.DeviceIdType.MESH,
        )

    def big_move(kind, source, slot, other):
        return remote(
            source, bigs[kind].at[slot], big_send.at[kind, slot], big_recv.at[kind, slot], other
        )

    def big_arrived(kind, slot):
        big_move(kind, bigs[kind].at[slot], slot, sibling).wait_recv()

    for kind, own in ((0, tok), (1, cot)):
        big_move(kind, own, 2, right).start()
        big_move(kind, own, 3, left).start()
        big_move(kind, own, 1, sibling).start()

    def piece_to(kind, source, target, other):
        return remote(
            source.at[other],
            target.at[me],
            piece_send.at[kind, other],
            piece_recv.at[kind, me],
            other,
        )

    def piece_from(kind, source, target, other):
        return remote(
            source.at[other],
            target.at[other],
            piece_send.at[kind, other],
            piece_recv.at[kind, other],
            other,
        )

    def each_other(act):
        def body(k, carry):
            act(lax.rem(me + k, devices))
            return carry

        lax.fori_loop(1, devices, body, 0)

    def gain_to(other):
        return remote(
            sent_gain.at[other], gain.at[me], gain_send.at[other], gain_recv.at[me], other
        )

    def gain_from(other):
        return remote(
            sent_gain.at[other], gain.at[other], gain_send.at[other], gain_recv.at[other], other
        )

    def hand_out(k, carry):
        other = lax.rem(me + k, devices)
        expert = held_by[other]
        sent_master[other] = master[expert].astype(jnp.bfloat16)
        named = jnp.sum(
            jnp.where(ids[...] == expert, gains_in[...], 0.0), axis=0, keepdims=True
        )
        sent_gain[other] = jnp.broadcast_to(named, sent_gain.shape[1:])

        @pl.when(k < devices)
        def _():
            piece_to(2, sent_master, got_master, other).start()
            gain_to(other).start()

        return carry

    lax.fori_loop(1, devices + 1, hand_out, 0)
    got_master[me] = sent_master[me]
    gain[me] = sent_gain[me]
    held_tok[0] = tok[...]
    held_cot[0] = cot[...]
    gradients = (out_a_in, out_b_in, out_a_out, out_b_out)
    for out in gradients:
        out[...] = jnp.zeros_like(out)
    each_other(lambda other: piece_from(2, sent_master, got_master, other).wait_recv())
    each_other(lambda other: gain_from(other).wait_recv())
    restore(got_master, flat, (a_in, b_in, a_out, b_out))
    loads[0].wait()
    loads[1].wait()

    def cut(slot, kind):
        return held.at[slot, pl.ds(part * kind, part)]

    def row_move(source, slot, kind, other):
        return remote(
            source, cut(slot, kind), row_send.at[kind, slot], row_recv.at[kind, slot], other
        )

    def row_arrived(slot, kind):
        row_move(cut(slot, kind), slot, kind, sibling).wait_recv()

    def gain_of(source, start, size):
        return column(gain[source][0:1, start : start + size])

    def start_rows():
        for kind in (0, 1):
            own = rows_in.at[pl.ds(part * kind, part)]
            row_move(own, 4, kind, right).start()
            row_move(own, 5, kind, left).start()
            row_move(own, 2, kind, sibling).start()

    def learn(tile, first, second):
        count, width = tok.shape
        pair = pl.ds(2 * tile, 2)
        rows = held_tok[pair].reshape(2 * count, width)
        gains = jnp.concatenate([gain_of(first, 0, count), gain_of(second, 0, count)], axis=0)
        grad = (gains * held_cot[pair].reshape(2 * count, width).astype(jnp.float32)).astype(
            jnp.bfloat16
        )
        mid_in = product(rows, a_in[...]).astype(jnp.bfloat16)
        joined = product(rows, wf[...]) + adapter_scale_factor * product(mid_in, b_in[...])
        gate = joined[:, :FF]
        up_part = joined[:, FF:]
        sigma = jax.nn.sigmoid(gate)
        active = gate * sigma
        hidden = (active * up_part).astype(jnp.bfloat16)
        mid_out = product(hidden, a_out[...]).astype(jnp.bfloat16)
        out_b_out[...] += adapter_scale_factor * outer(mid_out, grad)
        back_mid = (adapter_scale_factor * times_transposed(grad, b_out[...])).astype(jnp.bfloat16)
        out_a_out[...] += outer(back_mid, hidden)
        back_hidden = times_transposed(grad, wd[...]) + times_transposed(back_mid, a_out[...])
        back_gate = back_hidden * up_part * sigma * (1.0 + gate * (1.0 - sigma))
        back_up = back_hidden * active
        back_joined = jnp.concatenate([back_gate, back_up], axis=1).astype(jnp.bfloat16)
        out_b_in[...] += adapter_scale_factor * outer(mid_in, back_joined)
        back_in = (adapter_scale_factor * times_transposed(back_joined, b_in[...])).astype(
            jnp.bfloat16
        )
        out_a_in[...] += outer(back_in, rows)

    def step(s, carry):
        slot0 = 4 * s - 2

        @pl.when(s == 0)
        def _():
            for kind in (0, 1):
                big_arrived(kind, 1)

        @pl.when((s > 0) & (s < half))
        def _():
            for kind in (0, 1):
                for way, onward in ((0, right), (1, left)):
                    slot = slot0 + way
                    big_arrived(kind, slot)

                    @pl.when(s < half - 1)
                    def _():
                        big_move(kind, bigs[kind].at[slot], slot + 4, onward).start()

                    if way == kind:

                        @pl.when(s == half - 1)
                        def _():
                            big_move(kind, bigs[kind].at[slot], 4 * half - 2, onward).start()

                    big_move(kind, bigs[kind].at[slot], slot + 2, sibling).start()

            @pl.when(s == half - 1)
            def _():
                start_rows()

            for kind in (0, 1):
                for way in (0, 1):
                    big_arrived(kind, slot0 + 2 + way)

        @pl.when(s == half)
        def _():
            for kind in (0, 1):
                big_arrived(kind, slot0)
                big_move(kind, bigs[kind].at[slot0], slot0 + 1, sibling).start()
            for kind in (0, 1):
                big_arrived(kind, slot0 + 1)

        single = (s == 0) | (s == half)
        from_left = 2 * chip_at(place - s)
        from_right = 2 * chip_at(place + s)

        def tile_of(j, inner):
            which = core + j - 2 * core * j
            second = jnp.where(single, from_left + 1 - core, from_right + which)
            learn(jnp.where(s == 0, 0, 2 * s - 1) + j, from_left + which, second)
            return inner

        lax.fori_loop(0, jnp.where(single, 1, 2), tile_of, 0)
        return carry

    lax.fori_loop(0, half + 1, step, 0)

    flatten(gradients, flat, grads)
    each_other(lambda other: piece_to(0, grads, got_grads, other).start())
    held[0] = rows_in[...]
    got_grads[me] = grads[me]
    def row_step(s, carry):
        for kind in (0, 1):
            for way, onward in ((0, right), (1, left)):
                slot = 4 * s + way
                row_arrived(slot, kind)

                @pl.when(s < half - 1)
                def _():
                    row_move(cut(slot, kind), slot + 4, kind, onward).start()

                if way == kind:

                    @pl.when(s == half - 1)
                    def _():
                        row_move(cut(slot, kind), 1, kind, onward).start()

                row_move(cut(slot, kind), slot + 2, kind, sibling).start()
        return carry

    lax.fori_loop(1, half - 1, row_step, 0)
    loads[2].wait()
    loads[3].wait()
    each_other(lambda other: piece_from(0, grads, got_grads, other).wait_recv())

    def renew(k, carry):
        other = lax.rem(me + k, devices)
        expert = held_by[other]
        fresh[other] = adamw(
            master[expert], moment[expert], second[expert], got_grads[other].astype(jnp.float32)
        )
        serving[other] = fresh[other].astype(jnp.bfloat16)

        @pl.when(k < devices)
        def _():
            piece_to(1, serving, pieces, other).start()

        return carry

    lax.fori_loop(1, devices + 1, renew, 0)
    pieces[me] = serving[me]

    lax.fori_loop(half - 1, half, row_step, 0)

    def write_back(expert, carry):
        updated[expert] = fresh[owner[expert]]
        return carry

    lax.fori_loop(0, devices, write_back, 0)
    for kind in (0, 1):
        row_arrived(1, kind)
        row_move(cut(1, kind), 3, kind, sibling).start()

    def rest(slot, carry):
        for kind in (0, 1):
            row_arrived(slot, kind)
        return carry

    lax.fori_loop(2, 4, rest, 0)
    for s in range(1, half):
        lax.fori_loop(4 * s + 2, 4 * s + 4, rest, 0)

    def base_of(tile, carry):
        rows = held[pl.ds(8 * tile, 8)].reshape(8 * count, rows_in.shape[1])
        base[tile] = product(rows, wf[...])
        return carry

    lax.fori_loop(0, devices // 8, base_of, 0)
    each_other(lambda other: piece_from(1, serving, pieces, other).wait_recv())
    restore(pieces, flat, (a_in, b_in, a_out, b_out))

    def answer(k, carry):
        s = jnp.where(k == 0, 0, half - k)
        rows = held[pl.ds(4 * s, 4)].reshape(4 * count, rows_in.shape[1])
        mid_in = product(rows, a_in[...]).astype(jnp.bfloat16)
        from_base = base[s // 2, pl.ds(lax.rem(s, 2) * 4 * count, 4 * count), :]
        joined = from_base + adapter_scale_factor * product(mid_in, b_in[...])
        gate = joined[:, :FF]
        hidden = (gate * jax.nn.sigmoid(gate) * joined[:, FF:]).astype(jnp.bfloat16)
        mid_out = product(hidden, a_out[...]).astype(jnp.bfloat16)
        result = product(hidden, wd[...]) + adapter_scale_factor * product(mid_out, b_out[...])
        result = result.astype(jnp.bfloat16).astype(jnp.float32)
        first = 2 * chip_at(place - s)
        second_chip = 2 * chip_at(place + jnp.where(s == 0, half, s))
        gains = jnp.concatenate(
            [
                gain_of(first + core, tok.shape[0], count),
                gain_of(second_chip + core, tok.shape[0], count),
                gain_of(first + 1 - core, tok.shape[0], count),
                gain_of(second_chip + 1 - core, tok.shape[0], count),
            ],
            axis=0,
        )
        result = (gains * result).reshape(4, count, rows_in.shape[1])
        keep[s] = result[:2]
        give[s] = result[2:].astype(jnp.bfloat16)
        remote(give.at[s], got.at[s], give_send.at[s], give_recv.at[s], sibling).start()
        return carry

    lax.fori_loop(0, half, answer, 0)

    def sum_move(way, t, piece, other):
        spot = pl.ds(part * piece, part)
        return remote(
            out_buf.at[way, t, spot],
            in_buf.at[way, t, spot],
            sum_send.at[way, t, piece],
            sum_recv.at[way, t, piece],
            other,
        )

    def got_wait(s):
        remote(give.at[s], got.at[s], give_send.at[s], give_recv.at[s], sibling).wait_recv()

    def of_chip(s, way):
        return keep[s, way] + got[s, way].astype(jnp.float32)

    got_wait(0)
    opposite = of_chip(0, 1).astype(jnp.bfloat16)
    for way, onward in ((0, right), (1, left)):
        out_buf[way, 0, part * way : part * (way + 1), :] = opposite[part * way : part * (way + 1)]
        sum_move(way, 0, way, onward).start()
    for t in range(1, half):
        s = half - t
        got_wait(s)
        for way, onward in ((0, right), (1, left)):
            total = of_chip(s, 1 - way)
            for piece in (0, 1):
                low, high = part * piece, part * (piece + 1)
                term = total[low:high]
                if t > 1 or piece == way:
                    sum_move(way, t - 1, piece, onward).wait_recv()
                    term = term + in_buf[way, t - 1, low:high, :].astype(jnp.float32)
                out_buf[way, t, low:high, :] = term.astype(jnp.bfloat16)
                sum_move(way, t, piece, onward).start()
    total = of_chip(0, 0)
    for way in (0, 1):
        for piece in (0, 1):
            sum_move(way, half - 1, piece, left).wait_recv()
        total = total + in_buf[way, half - 1].astype(jnp.float32)
    decoded[...] = total.astype(jnp.bfloat16)

    def piece_sent(other):
        piece_to(0, grads, got_grads, other).wait_send()
        piece_to(1, serving, pieces, other).wait_send()
        piece_to(2, sent_master, got_master, other).wait_send()
        gain_to(other).wait_send()

    each_other(piece_sent)

    def rows_sent(slot, carry):
        for kind in (0, 1):
            row_move(cut(slot, kind), slot, kind, sibling).wait_send()
            big_move(kind, bigs[kind].at[slot], slot, sibling).wait_send()
        return carry

    lax.fori_loop(1, devices, rows_sent, 0)
    for s in range(half):
        remote(give.at[s], got.at[s], give_send.at[s], give_recv.at[s], sibling).wait_send()
    for way in (0, 1):
        for t in range(half):
            for piece in (0, 1):
                if t > 0 or piece == way:
                    sum_move(way, t, piece, left).wait_send()


def job(owner, held_by, tokens, cotangent, ids, gains, rows, master, moment, second, wf, wd):
    devices = lax.axis_size("ep")
    half = devices // 4
    count, width = rows.shape
    lane_rows = master.shape[1] // 128
    cube = (devices, lane_rows, 128)
    blocks = (devices,) + tokens.shape
    vmem = pl.BlockSpec(memory_space=pltpu.VMEM)
    smem = pl.BlockSpec(memory_space=pltpu.SMEM)
    anywhere = pl.BlockSpec(memory_space=pl.ANY)
    bf, f32 = jnp.bfloat16, jnp.float32
    sems = pltpu.SemaphoreType.DMA
    updated, decoded = pl.pallas_call(
        job_kernel,
        out_shape=(jax.ShapeDtypeStruct(cube, f32), jax.ShapeDtypeStruct((count, width), bf)),
        in_specs=[smem] * 2 + [vmem] * 6 + [anywhere] * 4,
        out_specs=(vmem,) * 2,
        scratch_shapes=[
            pltpu.VMEM(wf.shape, bf),
            pltpu.VMEM(wd.shape, bf),
            pltpu.VMEM(cube, f32),
            pltpu.VMEM(cube, f32),
            pltpu.VMEM(blocks, bf),
            pltpu.VMEM(blocks, bf),
            pltpu.VMEM((devices,) + gains.shape, f32),
            pltpu.VMEM((devices,) + gains.shape, f32),
            pltpu.VMEM(cube, bf),
            pltpu.VMEM(cube, bf),
            pltpu.VMEM(cube, bf),
            pltpu.VMEM((RANK, width), f32),
            pltpu.VMEM((RANK, 2 * FF), f32),
            pltpu.VMEM((RANK, FF), f32),
            pltpu.VMEM((RANK, width), f32),
            pltpu.VMEM(cube, bf),
            pltpu.VMEM(cube, f32),
            pltpu.VMEM(cube, bf),
            pltpu.VMEM(cube, bf),
            pltpu.VMEM((devices * lane_rows, 128), f32),
            pltpu.VMEM((width, RANK), bf),
            pltpu.VMEM((RANK, 2 * FF), bf),
            pltpu.VMEM((FF, RANK), bf),
            pltpu.VMEM((RANK, width), bf),
            pltpu.VMEM((devices, count, width), bf),
            pltpu.VMEM((devices // 8, 8 * count, 2 * FF), f32),
            pltpu.VMEM((half, 2, count, width), f32),
            pltpu.VMEM((half, 2, count, width), bf),
            pltpu.VMEM((half, 2, count, width), bf),
            pltpu.VMEM((2, half, count, width), bf),
            pltpu.VMEM((2, half, count, width), bf),
            sems((4,)),
            sems((2, devices)),
            sems((2, devices)),
            sems((devices,)),
            sems((devices,)),
            sems((3, devices)),
            sems((3, devices)),
            sems((2, devices)),
            sems((2, devices)),
            sems((half,)),
            sems((half,)),
            sems((2, half, 2)),
            sems((2, half, 2)),
        ],
        compiler_params=pltpu.CompilerParams(
            collective_id=0, has_side_effects=True, vmem_limit_bytes=60 * 1024 * 1024
        ),
        name="job",
    )(
        owner,
        held_by,
        tokens,
        cotangent,
        ids,
        gains,
        rows,
        master.reshape(cube),
        moment.reshape(cube),
        second.reshape(cube),
        wf,
        wd,
    )
    return updated.reshape(master.shape), decoded


def expert_decode(rows, joined_weight, down_weight, flat_bf):
    a_in, b_in, a_out, b_out = unpack(flat_bf)
    mid_in = product(rows, a_in).astype(jnp.bfloat16)
    joined = product(rows, joined_weight) + adapter_scale_factor * product(mid_in, b_in)
    gate = joined[:, :FF]
    hidden = (jax.nn.silu(gate) * joined[:, FF:]).astype(jnp.bfloat16)
    mid_out = product(hidden, a_out).astype(jnp.bfloat16)
    return (
        product(hidden, down_weight) + adapter_scale_factor * product(mid_out, b_out)
    ).astype(jnp.bfloat16)


def adamw(master, moment, second, grads):
    moment_new = beta_one * moment + (1.0 - beta_one) * grads
    second_new = beta_two * second + (1.0 - beta_two) * grads * grads
    step_size = moment_new / bias_one / (jnp.sqrt(second_new / bias_two) + epsilon)
    return master - learn_rate * (step_size + decay_rate * master)


def expert_weights(ids, weights, held_by):
    hit = ids[:, :, None] == held_by[None, None, :]
    return jnp.sum(jnp.where(hit, weights[:, :, None], 0.0), axis=1)


def exchange(array):
    return lax.all_to_all(array, "ep", split_axis=0, concat_axis=0, tiled=True)


def on_device(
    tokens,
    cotangent,
    route_ids,
    route_weights,
    owner,
    base_joined,
    base_down,
    master,
    moment,
    second,
    step_rows,
    step_ids,
    step_weights,
):
    experts = owner.shape[0]
    width = tokens.shape[1]
    me = lax.axis_index("ep")
    joined_weight = base_joined[0]
    down_weight = base_down[0]
    labels = jnp.arange(experts, dtype=jnp.int32)
    held_by = jnp.sum(jnp.where(owner[None, :] == labels[:, None], labels[None, :], 0), axis=1)
    steps, dec_rows = step_rows.shape[:2]

    tok_rows = tokens.shape[0]
    flat_rows = step_rows.reshape(steps * dec_rows, width)
    if experts == 16:
        def to_lanes(first, last):
            both = jnp.concatenate([first, last.reshape(steps * dec_rows, -1)]).T
            return jnp.pad(both, ((0, 0), (0, -both.shape[1] % 128)))

        updated, decoded = job(
            owner,
            held_by,
            tokens,
            cotangent,
            to_lanes(route_ids, step_ids),
            to_lanes(route_weights, step_weights),
            flat_rows,
            master,
            moment,
            second,
            joined_weight,
            down_weight,
        )
        return (updated, decoded.reshape(steps, dec_rows, width))

    def gather(array):
        return lax.all_gather(array, "ep", axis=0, tiled=True)

    my_weights = jnp.concatenate(
        [
            expert_weights(route_ids, route_weights, held_by),
            expert_weights(
                step_ids.reshape(steps * dec_rows, -1),
                step_weights.reshape(steps * dec_rows, -1),
                held_by,
            ),
        ]
    )
    all_weights = exchange(my_weights.T[:, None, :])[:, 0, :]
    chunks = max(1, experts // 16)
    part = tok_rows // chunks
    flat_bf = exchange(jnp.take(master.astype(jnp.bfloat16), held_by, axis=0)).reshape(-1)
    grads = 0.0
    for chunk in range(chunks):
        cut = slice(chunk * part, (chunk + 1) * part)
        all_tokens = gather(tokens[cut])
        all_cot = gather(cotangent[cut]).astype(jnp.float32)
        scaled = (all_weights[:, cut].reshape(-1, 1) * all_cot).astype(jnp.bfloat16)
        grads += expert_grads(all_tokens, scaled, joined_weight, down_weight, flat_bf)
    all_steps = gather(step_rows.reshape(steps * dec_rows, width))
    returned = exchange(grads.astype(jnp.bfloat16).reshape(experts, -1))
    my_grads = jnp.take(returned, owner, axis=0).astype(jnp.float32)
    updated = adamw(master, moment, second, my_grads)
    serving = exchange(jnp.take(updated.astype(jnp.bfloat16), held_by, axis=0)).reshape(-1)
    result = expert_decode(all_steps, joined_weight, down_weight, serving)
    back = exchange(result.reshape(experts, steps * dec_rows, width))
    mixed = jnp.sum(
        my_weights[tok_rows:].T[:, :, None] * back.astype(jnp.float32), axis=0
    )
    return (updated, mixed.astype(jnp.bfloat16).reshape(steps, dec_rows, width))


def solution(mesh):
    in_specs = (
        P(("grp", "ep"), None),
        P(("grp", "ep"), None),
        P(("grp", "ep"), None),
        P(("grp", "ep"), None),
        P("grp"),
        P("ep", None, None),
        P("ep", None, None),
        P("grp", "ep"),
        P("grp", "ep"),
        P("grp", "ep"),
        P(None, ("grp", "ep"), None),
        P(None, ("grp", "ep"), None),
        P(None, ("grp", "ep"), None),
    )
    out_specs = (P("grp", "ep"), P(None, ("grp", "ep"), None))
    return jax.shard_map(
        on_device, mesh=mesh, in_specs=in_specs, out_specs=out_specs, check_vma=False
    )
```

```python
import jax
import jax.numpy as jnp
from jax import lax
from jax.experimental import pallas as pl
from jax.experimental.pallas import tpu as pltpu
from jax.sharding import PartitionSpec as P

D = 2048
FF = 384
RANK = 32


adapter_scale_factor = 0.5
learn_rate = 0.05
beta_one = 0.9
beta_two = 0.999
decay_rate = 0.1
epsilon = 1e-08
bias_one = 1.0 - 0.9**50
bias_two = 1.0 - 0.999**50


def product(left, right):
    return jnp.dot(left, right, preferred_element_type=jnp.float32)


def unpack(flat):
    cut_one = D * RANK
    cut_two = cut_one + RANK * 2 * FF
    cut_three = cut_two + FF * RANK
    a_in = flat[:cut_one].reshape(D, RANK)
    b_in = flat[cut_one:cut_two].reshape(RANK, 2 * FF)
    a_out = flat[cut_two:cut_three].reshape(FF, RANK)
    b_out = flat[cut_three:].reshape(RANK, D)
    return (a_in, b_in, a_out, b_out)


def expert_grads(rows, grad_rows, joined_weight, down_weight, flat_bf):
    a_in, b_in, a_out, b_out = unpack(flat_bf)
    mid_in = product(rows, a_in).astype(jnp.bfloat16)
    joined = product(rows, joined_weight) + adapter_scale_factor * product(mid_in, b_in)
    gate = joined[:, :FF]
    up_part = joined[:, FF:]
    sigma = jax.nn.sigmoid(gate)
    active = gate * sigma
    hidden = (active * up_part).astype(jnp.bfloat16)
    mid_out = product(hidden, a_out).astype(jnp.bfloat16)
    grad_b_out = adapter_scale_factor * product(mid_out.T, grad_rows)
    back_mid = (adapter_scale_factor * product(grad_rows, b_out.T)).astype(jnp.bfloat16)
    grad_a_out = product(hidden.T, back_mid)
    back_hidden = product(grad_rows, down_weight.T) + product(back_mid, a_out.T)
    back_gate = back_hidden * up_part * sigma * (1.0 + gate * (1.0 - sigma))
    back_up = back_hidden * active
    back_joined = jnp.concatenate([back_gate, back_up], axis=1).astype(jnp.bfloat16)
    grad_b_in = adapter_scale_factor * product(mid_in.T, back_joined)
    back_in = (adapter_scale_factor * product(back_joined, b_in.T)).astype(jnp.bfloat16)
    grad_a_in = product(rows.T, back_in)
    return jnp.concatenate(
        [
            grad_a_in.reshape(-1),
            grad_b_in.reshape(-1),
            grad_a_out.reshape(-1),
            grad_b_out.reshape(-1),
        ]
    )


def snake(devices):
    chips = devices // 2
    half = chips // 2
    me = lax.axis_index("ep")
    core = lax.rem(me, 2)
    chip = me // 2
    place = jnp.where(lax.rem(chip, 2) == 0, chip // 2, chips - 1 - chip // 2)

    def chip_at(position):
        position = lax.rem(position + 2 * chips, chips)
        return jnp.where(position < half, 2 * position, 2 * (chips - 1 - position) + 1)

    return me, core, chip, place, chip_at


def spread(block):
    pieces = []
    for start in range(0, block.shape[0], 128):
        cut = block[start : start + 128]
        count = cut.shape[0]
        shape = (4 * count, count)
        rows = lax.broadcasted_iota(jnp.int32, shape, 0)
        repeat = (rows >> 2 == lax.broadcasted_iota(jnp.int32, shape, 1)).astype(jnp.bfloat16)
        wide = product(repeat, cut)
        shape = (4 * count, 128)
        rows = lax.broadcasted_iota(jnp.int32, shape, 0)
        lanes = lax.broadcasted_iota(jnp.int32, shape, 1)
        wide = jnp.where(lanes >> 5 == rows & 3, wide, 0.0).astype(jnp.bfloat16)
        shape = (128, RANK)
        lanes = lax.broadcasted_iota(jnp.int32, shape, 0)
        fold = (lanes & (RANK - 1) == lax.broadcasted_iota(jnp.int32, shape, 1)).astype(
            jnp.bfloat16
        )
        pieces.append(product(wide, fold).astype(jnp.bfloat16))
    return jnp.concatenate(pieces, axis=0)


def weave(block):
    count = block.shape[0]
    times = count // RANK
    shape = (count, count)
    rows = lax.broadcasted_iota(jnp.int32, shape, 0)
    source = (rows & (RANK - 1)) * times + (rows >> 5)
    pick = (source == lax.broadcasted_iota(jnp.int32, shape, 1)).astype(jnp.bfloat16)
    sorted_rows = product(pick, block).astype(jnp.bfloat16)
    return jnp.concatenate(
        [sorted_rows[RANK * j : RANK * (j + 1)] for j in range(times)], axis=1
    )


def unspread(block):
    pieces = []
    for start in range(0, block.shape[1], 512):
        cut = block[:, start : start + 512]
        count = cut.shape[1]
        shape = (RANK, 128)
        rows = lax.broadcasted_iota(jnp.int32, shape, 0)
        lanes = lax.broadcasted_iota(jnp.int32, shape, 1)
        tile = (lanes & (RANK - 1) == rows).astype(jnp.bfloat16)
        wide = outer(cut, tile)
        shape = (count, 128)
        rows = lax.broadcasted_iota(jnp.int32, shape, 0)
        lanes = lax.broadcasted_iota(jnp.int32, shape, 1)
        wide = jnp.where(lanes >> 5 == rows & 3, wide, 0.0).astype(jnp.bfloat16)
        shape = (count // 4, count)
        rows = lax.broadcasted_iota(jnp.int32, shape, 0)
        collapse = (rows == lax.broadcasted_iota(jnp.int32, shape, 1) >> 2).astype(jnp.bfloat16)
        pieces.append(product(collapse, wide))
    return jnp.concatenate(pieces, axis=0)


def unweave(block):
    times = block.shape[1] // 128
    stacked = jnp.concatenate([block[:, 128 * j : 128 * (j + 1)] for j in range(times)], axis=0)
    shape = (RANK * times, RANK * times)
    stack = lax.broadcasted_iota(jnp.int32, shape, 1)
    target = (stack & (RANK - 1)) * times + (stack >> 5)
    pick = (target == lax.broadcasted_iota(jnp.int32, shape, 0)).astype(jnp.bfloat16)
    return product(pick, stacked)


def flatten(gradients, flat, pieces):
    start = 0
    for grad, undo in zip(gradients, (unspread, unweave, unspread, unweave)):
        rows = undo(grad[...].astype(jnp.bfloat16))
        flat[start : start + rows.shape[0], :] = rows
        start += rows.shape[0]
    count = pieces.shape[1]
    for j in range(pieces.shape[0]):
        pieces[j] = flat[count * j : count * (j + 1), :].astype(jnp.bfloat16)


def outer(left_op, right_op):
    return lax.dot_general(
        left_op, right_op, (((0,), (0,)), ((), ())), preferred_element_type=jnp.float32
    )


def times_transposed(left_op, right_op):
    return lax.dot_general(
        left_op, right_op, (((1,), (1,)), ((), ())), preferred_element_type=jnp.float32
    )


def column(row):
    shape = (row.shape[1], row.shape[1])
    same = lax.broadcasted_iota(jnp.int32, shape, 0) == lax.broadcasted_iota(jnp.int32, shape, 1)
    return jnp.sum(jnp.where(same, row, 0.0), axis=1, keepdims=True)


def to_cube(table, cube):
    for j in range(cube.shape[1]):
        cube[:, j, :] = table[:, 128 * j : 128 * (j + 1)]


def to_table(cube, table):
    for j in range(cube.shape[1]):
        table[:, 128 * j : 128 * (j + 1)] = cube[:, j, :]


def restore(pieces, flat, factors):
    count = pieces.shape[1]
    for j in range(pieces.shape[0]):
        flat[count * j : count * (j + 1), :] = pieces[j].astype(jnp.float32)
    cuts = [0]
    for size in (D * RANK, RANK * 2 * FF, FF * RANK, RANK * D):
        cuts.append(cuts[-1] + size // 128)
    for k, undo in enumerate((spread, weave, spread, weave)):
        factors[k][...] = undo(flat[cuts[k] : cuts[k + 1], :].astype(jnp.bfloat16))


def job_kernel(
    owner,
    held_by,
    tok,
    cot,
    ids,
    gains_in,
    rows_in,
    master_in,
    moment_in,
    second_in,
    wf_in,
    wd_in,
    updated,
    decoded,
    wf,
    wd,
    moment_table,
    second_table,
    master,
    moment,
    second,
    held_tok,
    held_cot,
    sent_gain,
    gain,
    sent_master,
    got_master,
    grads,
    out_a_in,
    out_b_in,
    out_a_out,
    out_b_out,
    got_grads,
    fresh,
    serving,
    pieces,
    flat,
    a_in,
    b_in,
    a_out,
    b_out,
    held,
    base,
    keep,
    give,
    got,
    out_buf,
    in_buf,
    load_sem,
    big_send,
    big_recv,
    gain_send,
    gain_recv,
    piece_send,
    piece_recv,
    row_send,
    row_recv,
    give_send,
    give_recv,
    sum_send,
    sum_recv,
):
    devices = lax.axis_size("ep")
    half = devices // 4
    me, core, chip, place, chip_at = snake(devices)
    right = 2 * chip_at(place + 1) + core
    left = 2 * chip_at(place - 1) + core
    sibling = 2 * chip + 1 - core
    count = rows_in.shape[0]
    part = count // 2

    loads = [
        pltpu.make_async_copy(source, target, load_sem.at[k])
        for k, (source, target) in enumerate(
            ((wf_in, wf), (wd_in, wd), (moment_in, moment_table), (second_in, second_table))
        )
    ]
    for load in loads:
        load.start()
    bigs = (held_tok, held_cot)
    barrier = pltpu.get_barrier_semaphore()

    def greet(k, carry):
        pl.semaphore_signal(
            barrier,
            inc=1,
            device_id={"ep": lax.rem(me + k, devices)},
            device_id_type=pl.DeviceIdType.MESH,
        )
        return carry

    lax.fori_loop(1, devices, greet, 0)
    pl.semaphore_wait(barrier, devices - 1)

    def remote(source, target, send, recv, other):
        return pltpu.make_async_remote_copy(
            src_ref=source,
            dst_ref=target,
            send_sem=send,
            recv_sem=recv,
            device_id={"ep": other},
            device_id_type=pl.DeviceIdType.MESH,
        )

    def big_move(kind, source, slot, other):
        return remote(
            source, bigs[kind].at[slot], big_send.at[kind, slot], big_recv.at[kind, slot], other
        )

    def big_arrived(kind, slot):
        big_move(kind, bigs[kind].at[slot], slot, sibling).wait_recv()

    for kind, own in ((0, tok), (1, cot)):
        big_move(kind, own, 2, right).start()
        big_move(kind, own, 3, left).start()
        big_move(kind, own, 1, sibling).start()

    def piece_to(kind, source, target, other):
        return remote(
            source.at[other],
            target.at[me],
            piece_send.at[kind, other],
            piece_recv.at[kind, me],
            other,
        )

    def piece_from(kind, source, target, other):
        return remote(
            source.at[other],
            target.at[other],
            piece_send.at[kind, other],
            piece_recv.at[kind, other],
            other,
        )

    def each_other(act):
        def body(k, carry):
            act(lax.rem(me + k, devices))
            return carry

        lax.fori_loop(1, devices, body, 0)

    def gain_to(other):
        return remote(
            sent_gain.at[other], gain.at[me], gain_send.at[other], gain_recv.at[me], other
        )

    def gain_from(other):
        return remote(
            sent_gain.at[other], gain.at[other], gain_send.at[other], gain_recv.at[other], other
        )

    to_cube(master_in, master)

    def hand_out(k, carry):
        other = lax.rem(me + k, devices)
        expert = held_by[other]
        sent_master[other] = master[expert].astype(jnp.bfloat16)
        named = jnp.sum(
            jnp.where(ids[...] == expert, gains_in[...], 0.0), axis=0, keepdims=True
        )
        sent_gain[other] = jnp.broadcast_to(named, sent_gain.shape[1:])

        @pl.when(k < devices)
        def _():
            piece_to(2, sent_master, got_master, other).start()
            gain_to(other).start()

        return carry

    lax.fori_loop(1, devices + 1, hand_out, 0)
    got_master[me] = sent_master[me]
    gain[me] = sent_gain[me]
    held_tok[0] = tok[...]
    held_cot[0] = cot[...]
    gradients = (out_a_in, out_b_in, out_a_out, out_b_out)
    for out in gradients:
        out[...] = jnp.zeros_like(out)
    each_other(lambda other: piece_from(2, sent_master, got_master, other).wait_recv())
    each_other(lambda other: gain_from(other).wait_recv())
    restore(got_master, flat, (a_in, b_in, a_out, b_out))
    loads[0].wait()
    loads[1].wait()

    def cut(slot, kind):
        return held.at[slot, pl.ds(part * kind, part)]

    def row_move(source, slot, kind, other):
        return remote(
            source, cut(slot, kind), row_send.at[kind, slot], row_recv.at[kind, slot], other
        )

    def row_arrived(slot, kind):
        row_move(cut(slot, kind), slot, kind, sibling).wait_recv()

    def gain_of(source, start, size):
        return column(gain[source][0:1, start : start + size])

    def start_rows():
        for kind in (0, 1):
            own = rows_in.at[pl.ds(part * kind, part)]
            row_move(own, 4, kind, right).start()
            row_move(own, 5, kind, left).start()
            row_move(own, 2, kind, sibling).start()

    def learn(tile, first, second):
        count, width = tok.shape
        pair = pl.ds(2 * tile, 2)
        rows = held_tok[pair].reshape(2 * count, width)
        gains = jnp.concatenate([gain_of(first, 0, count), gain_of(second, 0, count)], axis=0)
        grad = (gains * held_cot[pair].reshape(2 * count, width).astype(jnp.float32)).astype(
            jnp.bfloat16
        )
        mid_in = product(rows, a_in[...]).astype(jnp.bfloat16)
        joined = product(rows, wf[...]) + adapter_scale_factor * product(mid_in, b_in[...])
        gate = joined[:, :FF]
        up_part = joined[:, FF:]
        sigma = jax.nn.sigmoid(gate)
        active = gate * sigma
        hidden = (active * up_part).astype(jnp.bfloat16)
        mid_out = product(hidden, a_out[...]).astype(jnp.bfloat16)
        out_b_out[...] += adapter_scale_factor * outer(mid_out, grad)
        back_mid = (adapter_scale_factor * times_transposed(grad, b_out[...])).astype(jnp.bfloat16)
        out_a_out[...] += outer(back_mid, hidden)
        back_hidden = times_transposed(grad, wd[...]) + times_transposed(back_mid, a_out[...])
        back_gate = back_hidden * up_part * sigma * (1.0 + gate * (1.0 - sigma))
        back_up = back_hidden * active
        back_joined = jnp.concatenate([back_gate, back_up], axis=1).astype(jnp.bfloat16)
        out_b_in[...] += adapter_scale_factor * outer(mid_in, back_joined)
        back_in = (adapter_scale_factor * times_transposed(back_joined, b_in[...])).astype(
            jnp.bfloat16
        )
        out_a_in[...] += outer(back_in, rows)

    def step(s, carry):
        slot0 = 4 * s - 2

        @pl.when(s == 0)
        def _():
            for kind in (0, 1):
                big_arrived(kind, 1)

        @pl.when((s > 0) & (s < half))
        def _():
            for kind in (0, 1):
                for way, onward in ((0, right), (1, left)):
                    slot = slot0 + way
                    big_arrived(kind, slot)

                    @pl.when(s < half - 1)
                    def _():
                        big_move(kind, bigs[kind].at[slot], slot + 4, onward).start()

                    if way == kind:

                        @pl.when(s == half - 1)
                        def _():
                            big_move(kind, bigs[kind].at[slot], 4 * half - 2, onward).start()

                    big_move(kind, bigs[kind].at[slot], slot + 2, sibling).start()

            @pl.when(s == 1)
            def _():
                loads[2].wait()
                loads[3].wait()
                to_cube(moment_table, moment)
                to_cube(second_table, second)

            @pl.when(s == half - 1)
            def _():
                start_rows()

            for kind in (0, 1):
                for way in (0, 1):
                    big_arrived(kind, slot0 + 2 + way)

        @pl.when(s == half)
        def _():
            for kind in (0, 1):
                big_arrived(kind, slot0)
                big_move(kind, bigs[kind].at[slot0], slot0 + 1, sibling).start()
            for kind in (0, 1):
                big_arrived(kind, slot0 + 1)

        single = (s == 0) | (s == half)
        from_left = 2 * chip_at(place - s)
        from_right = 2 * chip_at(place + s)

        def tile_of(j, inner):
            which = core + j - 2 * core * j
            second = jnp.where(single, from_left + 1 - core, from_right + which)
            learn(jnp.where(s == 0, 0, 2 * s - 1) + j, from_left + which, second)
            return inner

        lax.fori_loop(0, jnp.where(single, 1, 2), tile_of, 0)
        return carry

    lax.fori_loop(0, half + 1, step, 0)

    flatten(gradients, flat, grads)
    each_other(lambda other: piece_to(0, grads, got_grads, other).start())
    held[0] = rows_in[...]
    got_grads[me] = grads[me]
    def row_step(s, carry):
        for kind in (0, 1):
            for way, onward in ((0, right), (1, left)):
                slot = 4 * s + way
                row_arrived(slot, kind)

                @pl.when(s < half - 1)
                def _():
                    row_move(cut(slot, kind), slot + 4, kind, onward).start()

                if way == kind:

                    @pl.when(s == half - 1)
                    def _():
                        row_move(cut(slot, kind), 1, kind, onward).start()

                row_move(cut(slot, kind), slot + 2, kind, sibling).start()
        return carry

    lax.fori_loop(1, half - 1, row_step, 0)
    each_other(lambda other: piece_from(0, grads, got_grads, other).wait_recv())

    def renew(k, carry):
        other = lax.rem(me + k, devices)
        expert = held_by[other]
        fresh[other] = adamw(
            master[expert], moment[expert], second[expert], got_grads[other].astype(jnp.float32)
        )
        serving[other] = fresh[other].astype(jnp.bfloat16)

        @pl.when(k < devices)
        def _():
            piece_to(1, serving, pieces, other).start()

        return carry

    lax.fori_loop(1, devices + 1, renew, 0)
    pieces[me] = serving[me]

    lax.fori_loop(half - 1, half, row_step, 0)

    def write_back(expert, carry):
        master[expert] = fresh[owner[expert]]
        return carry

    lax.fori_loop(0, devices, write_back, 0)
    to_table(master, updated)
    for kind in (0, 1):
        row_arrived(1, kind)
        row_move(cut(1, kind), 3, kind, sibling).start()

    def rest(slot, carry):
        for kind in (0, 1):
            row_arrived(slot, kind)
        return carry

    lax.fori_loop(2, 4, rest, 0)
    for s in range(1, half):
        lax.fori_loop(4 * s + 2, 4 * s + 4, rest, 0)

    def base_of(tile, carry):
        rows = held[pl.ds(8 * tile, 8)].reshape(8 * count, rows_in.shape[1])
        base[tile] = product(rows, wf[...])
        return carry

    lax.fori_loop(0, devices // 8, base_of, 0)
    each_other(lambda other: piece_from(1, serving, pieces, other).wait_recv())
    restore(pieces, flat, (a_in, b_in, a_out, b_out))

    def answer(k, carry):
        s = jnp.where(k == 0, 0, half - k)
        rows = held[pl.ds(4 * s, 4)].reshape(4 * count, rows_in.shape[1])
        mid_in = product(rows, a_in[...]).astype(jnp.bfloat16)
        from_base = base[s // 2, pl.ds(lax.rem(s, 2) * 4 * count, 4 * count), :]
        joined = from_base + adapter_scale_factor * product(mid_in, b_in[...])
        gate = joined[:, :FF]
        hidden = (gate * jax.nn.sigmoid(gate) * joined[:, FF:]).astype(jnp.bfloat16)
        mid_out = product(hidden, a_out[...]).astype(jnp.bfloat16)
        result = product(hidden, wd[...]) + adapter_scale_factor * product(mid_out, b_out[...])
        result = result.astype(jnp.bfloat16).astype(jnp.float32)
        first = 2 * chip_at(place - s)
        second_chip = 2 * chip_at(place + jnp.where(s == 0, half, s))
        gains = jnp.concatenate(
            [
                gain_of(first + core, tok.shape[0], count),
                gain_of(second_chip + core, tok.shape[0], count),
                gain_of(first + 1 - core, tok.shape[0], count),
                gain_of(second_chip + 1 - core, tok.shape[0], count),
            ],
            axis=0,
        )
        result = (gains * result).reshape(4, count, rows_in.shape[1])
        keep[s] = result[:2]
        give[s] = result[2:].astype(jnp.bfloat16)
        remote(give.at[s], got.at[s], give_send.at[s], give_recv.at[s], sibling).start()
        return carry

    lax.fori_loop(0, 2, answer, 0)

    def sum_move(way, t, piece, other):
        spot = pl.ds(part * piece, part)
        return remote(
            out_buf.at[way, t, spot],
            in_buf.at[way, t, spot],
            sum_send.at[way, t, piece],
            sum_recv.at[way, t, piece],
            other,
        )

    def got_wait(s):
        remote(give.at[s], got.at[s], give_send.at[s], give_recv.at[s], sibling).wait_recv()

    def of_chip(s, way):
        return keep[s, way] + got[s, way].astype(jnp.float32)

    got_wait(0)
    opposite = of_chip(0, 1).astype(jnp.bfloat16)
    for way, onward in ((0, right), (1, left)):
        out_buf[way, 0, part * way : part * (way + 1), :] = opposite[part * way : part * (way + 1)]
        sum_move(way, 0, way, onward).start()
    for t in range(1, half):
        s = half - t
        if t > 1:
            lax.fori_loop(t, t + 1, answer, 0)
        got_wait(s)
        for way, onward in ((0, right), (1, left)):
            total = of_chip(s, 1 - way)
            for piece in (0, 1):
                low, high = part * piece, part * (piece + 1)
                term = total[low:high]
                if t > 1 or piece == way:
                    sum_move(way, t - 1, piece, onward).wait_recv()
                    term = term + in_buf[way, t - 1, low:high, :].astype(jnp.float32)
                out_buf[way, t, low:high, :] = term.astype(jnp.bfloat16)
                sum_move(way, t, piece, onward).start()
    total = of_chip(0, 0)
    for way in (0, 1):
        for piece in (0, 1):
            sum_move(way, half - 1, piece, left).wait_recv()
        total = total + in_buf[way, half - 1].astype(jnp.float32)
    decoded[...] = total.astype(jnp.bfloat16)

    def piece_sent(other):
        piece_to(0, grads, got_grads, other).wait_send()
        piece_to(1, serving, pieces, other).wait_send()
        piece_to(2, sent_master, got_master, other).wait_send()
        gain_to(other).wait_send()

    each_other(piece_sent)

    def rows_sent(slot, carry):
        for kind in (0, 1):
            row_move(cut(slot, kind), slot, kind, sibling).wait_send()
            big_move(kind, bigs[kind].at[slot], slot, sibling).wait_send()
        return carry

    lax.fori_loop(1, devices, rows_sent, 0)
    for s in range(half):
        remote(give.at[s], got.at[s], give_send.at[s], give_recv.at[s], sibling).wait_send()
    for way in (0, 1):
        for t in range(half):
            for piece in (0, 1):
                if t > 0 or piece == way:
                    sum_move(way, t, piece, left).wait_send()


def job(owner, held_by, tokens, cotangent, ids, gains, rows, master, moment, second, wf, wd):
    devices = lax.axis_size("ep")
    half = devices // 4
    count, width = rows.shape
    lane_rows = master.shape[1] // 128
    cube = (devices, lane_rows, 128)
    blocks = (devices,) + tokens.shape
    vmem = pl.BlockSpec(memory_space=pltpu.VMEM)
    smem = pl.BlockSpec(memory_space=pltpu.SMEM)
    anywhere = pl.BlockSpec(memory_space=pl.ANY)
    bf, f32 = jnp.bfloat16, jnp.float32
    sems = pltpu.SemaphoreType.DMA
    updated, decoded = pl.pallas_call(
        job_kernel,
        out_shape=(jax.ShapeDtypeStruct(master.shape, f32), jax.ShapeDtypeStruct((count, width), bf)),
        in_specs=[smem] * 2 + [vmem] * 6 + [anywhere] * 4,
        out_specs=(vmem,) * 2,
        scratch_shapes=[
            pltpu.VMEM(wf.shape, bf),
            pltpu.VMEM(wd.shape, bf),
            pltpu.VMEM(master.shape, f32),
            pltpu.VMEM(master.shape, f32),
            pltpu.VMEM(cube, f32),
            pltpu.VMEM(cube, f32),
            pltpu.VMEM(cube, f32),
            pltpu.VMEM(blocks, bf),
            pltpu.VMEM(blocks, bf),
            pltpu.VMEM((devices,) + gains.shape, f32),
            pltpu.VMEM((devices,) + gains.shape, f32),
            pltpu.VMEM(cube, bf),
            pltpu.VMEM(cube, bf),
            pltpu.VMEM(cube, bf),
            pltpu.VMEM((RANK, width), f32),
            pltpu.VMEM((RANK, 2 * FF), f32),
            pltpu.VMEM((RANK, FF), f32),
            pltpu.VMEM((RANK, width), f32),
            pltpu.VMEM(cube, bf),
            pltpu.VMEM(cube, f32),
            pltpu.VMEM(cube, bf),
            pltpu.VMEM(cube, bf),
            pltpu.VMEM((devices * lane_rows, 128), f32),
            pltpu.VMEM((width, RANK), bf),
            pltpu.VMEM((RANK, 2 * FF), bf),
            pltpu.VMEM((FF, RANK), bf),
            pltpu.VMEM((RANK, width), bf),
            pltpu.VMEM((devices, count, width), bf),
            pltpu.VMEM((devices // 8, 8 * count, 2 * FF), f32),
            pltpu.VMEM((half, 2, count, width), f32),
            pltpu.VMEM((half, 2, count, width), bf),
            pltpu.VMEM((half, 2, count, width), bf),
            pltpu.VMEM((2, half, count, width), bf),
            pltpu.VMEM((2, half, count, width), bf),
            sems((4,)),
            sems((2, devices)),
            sems((2, devices)),
            sems((devices,)),
            sems((devices,)),
            sems((3, devices)),
            sems((3, devices)),
            sems((2, devices)),
            sems((2, devices)),
            sems((half,)),
            sems((half,)),
            sems((2, half, 2)),
            sems((2, half, 2)),
        ],
        compiler_params=pltpu.CompilerParams(
            collective_id=0, has_side_effects=True, vmem_limit_bytes=60 * 1024 * 1024
        ),
        name="job",
    )(
        owner,
        held_by,
        tokens,
        cotangent,
        ids,
        gains,
        rows,
        master,
        moment,
        second,
        wf,
        wd,
    )
    return updated, decoded


def expert_decode(rows, joined_weight, down_weight, flat_bf):
    a_in, b_in, a_out, b_out = unpack(flat_bf)
    mid_in = product(rows, a_in).astype(jnp.bfloat16)
    joined = product(rows, joined_weight) + adapter_scale_factor * product(mid_in, b_in)
    gate = joined[:, :FF]
    hidden = (jax.nn.silu(gate) * joined[:, FF:]).astype(jnp.bfloat16)
    mid_out = product(hidden, a_out).astype(jnp.bfloat16)
    return (
        product(hidden, down_weight) + adapter_scale_factor * product(mid_out, b_out)
    ).astype(jnp.bfloat16)


def adamw(master, moment, second, grads):
    moment_new = beta_one * moment + (1.0 - beta_one) * grads
    second_new = beta_two * second + (1.0 - beta_two) * grads * grads
    step_size = moment_new / bias_one / (jnp.sqrt(second_new / bias_two) + epsilon)
    return master - learn_rate * (step_size + decay_rate * master)


def expert_weights(ids, weights, held_by):
    hit = ids[:, :, None] == held_by[None, None, :]
    return jnp.sum(jnp.where(hit, weights[:, :, None], 0.0), axis=1)


def exchange(array):
    return lax.all_to_all(array, "ep", split_axis=0, concat_axis=0, tiled=True)


def on_device(
    tokens,
    cotangent,
    route_ids,
    route_weights,
    owner,
    base_joined,
    base_down,
    master,
    moment,
    second,
    step_rows,
    step_ids,
    step_weights,
):
    experts = owner.shape[0]
    width = tokens.shape[1]
    me = lax.axis_index("ep")
    joined_weight = base_joined[0]
    down_weight = base_down[0]
    labels = jnp.arange(experts, dtype=jnp.int32)
    held_by = jnp.sum(jnp.where(owner[None, :] == labels[:, None], labels[None, :], 0), axis=1)
    steps, dec_rows = step_rows.shape[:2]

    tok_rows = tokens.shape[0]
    flat_rows = step_rows.reshape(steps * dec_rows, width)
    if experts == 16:
        def to_lanes(first, last):
            both = jnp.concatenate([first, last.reshape(steps * dec_rows, -1)]).T
            return jnp.pad(both, ((0, 0), (0, -both.shape[1] % 128)))

        updated, decoded = job(
            owner,
            held_by,
            tokens,
            cotangent,
            to_lanes(route_ids, step_ids),
            to_lanes(route_weights, step_weights),
            flat_rows,
            master,
            moment,
            second,
            joined_weight,
            down_weight,
        )
        return (updated, decoded.reshape(steps, dec_rows, width))

    def gather(array):
        return lax.all_gather(array, "ep", axis=0, tiled=True)

    my_weights = jnp.concatenate(
        [
            expert_weights(route_ids, route_weights, held_by),
            expert_weights(
                step_ids.reshape(steps * dec_rows, -1),
                step_weights.reshape(steps * dec_rows, -1),
                held_by,
            ),
        ]
    )
    all_weights = exchange(my_weights.T[:, None, :])[:, 0, :]
    chunks = max(1, experts // 16)
    part = tok_rows // chunks
    flat_bf = exchange(jnp.take(master.astype(jnp.bfloat16), held_by, axis=0)).reshape(-1)
    grads = 0.0
    for chunk in range(chunks):
        cut = slice(chunk * part, (chunk + 1) * part)
        all_tokens = gather(tokens[cut])
        all_cot = gather(cotangent[cut]).astype(jnp.float32)
        scaled = (all_weights[:, cut].reshape(-1, 1) * all_cot).astype(jnp.bfloat16)
        grads += expert_grads(all_tokens, scaled, joined_weight, down_weight, flat_bf)
    all_steps = gather(step_rows.reshape(steps * dec_rows, width))
    returned = exchange(grads.astype(jnp.bfloat16).reshape(experts, -1))
    my_grads = jnp.take(returned, owner, axis=0).astype(jnp.float32)
    updated = adamw(master, moment, second, my_grads)
    serving = exchange(jnp.take(updated.astype(jnp.bfloat16), held_by, axis=0)).reshape(-1)
    result = expert_decode(all_steps, joined_weight, down_weight, serving)
    back = exchange(result.reshape(experts, steps * dec_rows, width))
    mixed = jnp.sum(
        my_weights[tok_rows:].T[:, :, None] * back.astype(jnp.float32), axis=0
    )
    return (updated, mixed.astype(jnp.bfloat16).reshape(steps, dec_rows, width))


def solution(mesh):
    in_specs = (
        P(("grp", "ep"), None),
        P(("grp", "ep"), None),
        P(("grp", "ep"), None),
        P(("grp", "ep"), None),
        P("grp"),
        P("ep", None, None),
        P("ep", None, None),
        P("grp", "ep"),
        P("grp", "ep"),
        P("grp", "ep"),
        P(None, ("grp", "ep"), None),
        P(None, ("grp", "ep"), None),
        P(None, ("grp", "ep"), None),
    )
    out_specs = (P("grp", "ep"), P(None, ("grp", "ep"), None))
    return jax.shard_map(
        on_device, mesh=mesh, in_specs=in_specs, out_specs=out_specs, check_vma=False
    )
```
